32 devices in a mesh: seq: 8 (over z, y), head: 4 (over x, core).
Axes of the slice: x: 2, y: 2, z: 4, core: 2. Of those that a mesh axis runs over, the one named last changes fastest.
Arguments:
- queries: bfloat16 [4096, 2048], P('seq', 'head'), may hold values from -6 to 6
- key_vectors: bfloat16 [4096, 2048], P('seq', 'head'), may hold values from -6 to 6
- values: bfloat16 [4096, 4096], P('seq', 'head'), may hold values from -24 to 24
- gate_log: float32 [32, 4096], P('head', 'seq'), may hold values from -1 to 0
- write_rate: float32 [32, 4096], P('head', 'seq'), as said below
- prompt_stretches: int32 [4], replicated, may hold values from 1 to 32, as said below
- decode_owner: int32 [4], replicated, may hold values from 0 to 7, as said below
- norm_gain: float32 [128], replicated, may hold values from 0.25 to 1.75
- out_weight: bfloat16 [4096, 2048], P('head'), may hold values from -0.09375 to 0.09375
Outputs:
- mixed: bfloat16 [4096, 2048], P('seq', 'head')
- decode_states: float32 [8, 32, 128, 128], P('seq', 'head')
The draws below stay inside these ranges and needn't reach their ends.
Inputs may be any that keep to these rules, and one draw needn't show every extreme that they name: `prompt_stretches`: prompts lie in order along the token dimension, each a whole number of stretches of 64 tokens; the lengths sum to 64 and the longest is exactly 32. `decode_owner`: the 4 entries are distinct. `write_rate`: every entry is positive.
All inputs are finite; a program needn't handle non-finite values.
Results may differ from the reference program's by a relative error of at most 0.014.
Values may be sent and summed in bfloat16 or wider, within the bound.
A program may use at most 64 MiB of HBM per device.

```python
import math
import jax
import jax.numpy as jnp
from jax import lax

D_MODEL = 2048
HK = 16
VALUE_HEADS = 32
DK = 128
DV = 128
STRETCH = 64
PROMPTS = 4
PACKED_TOKENS = 4096
NCHUNKS = 64
LONGEST = 32
N_SEQ = 8
N_HEAD = 4


def slow_heads(key):
    share = 0.5
    return jax.random.uniform(jax.random.fold_in(key, 7), (VALUE_HEADS, 1), jnp.float32) < share


def draw_key_vectors(key, part):
    prompt_flows = jax.random.split(jax.random.fold_in(key, 31), 2)
    shared = jax.random.normal(prompt_flows[0], (NCHUNKS, 1, HK * DK), jnp.float32)
    noise = jax.random.normal(prompt_flows[1], (NCHUNKS, STRETCH, HK * DK), jnp.float32)
    combined = (3.0 * shared + noise) * 10.0 ** (-0.5)
    return jnp.clip(combined, -6.0, 6.0).reshape(PACKED_TOKENS, HK * DK).astype(jnp.bfloat16)


def draw_gate_log(key, part):
    prompt_flows = jax.random.split(jax.random.fold_in(key, 11), 5)
    interval_span = float(LONGEST * STRETCH)
    slow = slow_heads(key)
    slow_rate = jnp.exp(jax.random.uniform(prompt_flows[0], (VALUE_HEADS, 1), jnp.float32, math.log(0.05), math.log(0.3))) / interval_span
    fast_rate = jnp.exp(jax.random.uniform(prompt_flows[1], (VALUE_HEADS, 1), jnp.float32, math.log(0.0015), math.log(0.03)))
    head_write_speed = jnp.where(slow, slow_rate, fast_rate)
    random_wobble = jnp.exp(jax.random.uniform(prompt_flows[2], (VALUE_HEADS, PACKED_TOKENS), jnp.float32, math.log(0.5), math.log(2.0)))
    sudden_spike = jax.random.uniform(prompt_flows[3], (1, PACKED_TOKENS), jnp.float32) < 2.0 / interval_span
    spike_depth = jnp.log(jax.random.uniform(prompt_flows[4], (VALUE_HEADS, PACKED_TOKENS), jnp.float32, 0.5, 0.8))
    return -head_write_speed * random_wobble + jnp.where(sudden_spike, spike_depth, 0.0)


def draw_write_rate(key, part):
    prompt_flows = jax.random.split(jax.random.fold_in(key, 13), 2)
    slow = slow_heads(key)
    gentle = jax.random.uniform(prompt_flows[0], (VALUE_HEADS, PACKED_TOKENS), jnp.float32, 0.015, 0.045)
    strong = jax.random.uniform(prompt_flows[1], (VALUE_HEADS, PACKED_TOKENS), jnp.float32, 0.05, 0.95)
    return jnp.where(slow, gentle, strong)


def prompt_plan(key):
    prompt_flows = jax.random.split(jax.random.fold_in(key, 23), 3)
    others_total = NCHUNKS - LONGEST
    cuts = jax.random.permutation(prompt_flows[0], others_total - 1)[:PROMPTS - 2].astype(jnp.int32) + 1
    cuts = jnp.sort(cuts)
    bounds = jnp.concatenate([jnp.zeros((1,), jnp.int32), cuts, jnp.full((1,), others_total, jnp.int32)])
    others = bounds[1:] - bounds[:-1]
    longest_at = jax.random.randint(prompt_flows[1], (), 0, PROMPTS).astype(jnp.int32)
    index = jnp.arange(PROMPTS, dtype=jnp.int32)
    source = jnp.clip(jnp.where(index > longest_at, index - 1, index), 0, PROMPTS - 2)
    lengths = jnp.where(index == longest_at, LONGEST, others[source]).astype(jnp.int32)
    finish = jnp.cumsum(lengths).astype(jnp.int32)
    per_device = NCHUNKS // N_SEQ
    closer = (finish - 1) // per_device
    last_owner = jnp.remainder(closer[PROMPTS - 1] - 1, N_SEQ).astype(jnp.int32)
    partner = jnp.where(longest_at == PROMPTS - 1, PROMPTS - 2, longest_at).astype(jnp.int32)
    partner_owner = jnp.remainder(closer[partner] - N_SEQ // 2, N_SEQ).astype(jnp.int32)
    order = jax.random.permutation(prompt_flows[2], N_SEQ).astype(jnp.int32)
    spare = (order != last_owner) & (order != partner_owner)
    ranked = order[jnp.argsort(1 - spare.astype(jnp.int32), stable=True)]
    free_slot = (index != PROMPTS - 1) & (index != partner)
    rank = jnp.clip(jnp.cumsum(free_slot.astype(jnp.int32)) - 1, 0, N_SEQ - 1)
    owners = jnp.where(index == PROMPTS - 1, last_owner, jnp.where(index == partner, partner_owner, ranked[rank]))
    return (lengths, owners.astype(jnp.int32))


def draw_prompt_stretches(key, part):
    return prompt_plan(key)[0]


def draw_decode_owner(key, part):
    return prompt_plan(key)[1]


def block_scale(own_key, dims, shards, smallest, high):
    def one(dim, shards_of):
        heights = jax.random.uniform(jax.random.fold_in(jax.random.fold_in(own_key, 6), dim), (shards_of,), jnp.float32, smallest / len(shards), high / len(shards))
        return jnp.repeat(jnp.exp(heights), dims[dim] // shards_of).reshape((-1,) + (1,) * (len(dims) - dim - 1))

    gain = one(*shards[0])
    for cut in shards[1:]:
        gain = gain * one(*cut)
    return gain


def bell_draw(rng, dims, scale, limit, cuts=(), held_as=jnp.bfloat16):
    array = jax.random.normal(rng, dims, jnp.float32) * scale
    if len(cuts) > 0:
        array = block_scale(rng, dims, cuts, -0.22, 0.18) * array
    return jnp.clip(array, min=-limit, max=limit).astype(held_as)


def setup_inputs(seed: int = 0) -> dict:
    seeds = jax.random.split(jax.random.key(seed), 10)
    queries = bell_draw(seeds[0], (PACKED_TOKENS, HK * DK), 1.0, 6.0, ((0, 8), (1, 4)))
    key_vectors = draw_key_vectors(jax.random.fold_in(seeds[9], 71), 0)
    values = bell_draw(seeds[2], (PACKED_TOKENS, VALUE_HEADS * DV), 4.0, 24.0, ((0, 8), (1, 4)))
    gate_log = draw_gate_log(jax.random.fold_in(seeds[9], 71), 0)
    write_rate = draw_write_rate(jax.random.fold_in(seeds[9], 71), 0)
    prompt_stretches = draw_prompt_stretches(jax.random.fold_in(seeds[9], 71), 0)
    decode_owner = draw_decode_owner(jax.random.fold_in(seeds[9], 71), 0)
    norm_gain = jnp.clip(1.0 + 0.15 * jax.random.normal(seeds[7], (DV,), jnp.float32), 0.25, 1.75)
    out_weight = bell_draw(seeds[8], (VALUE_HEADS * DV, D_MODEL), (VALUE_HEADS * DV) ** -0.5, 0.09375, ((0, 4),))
    return dict(queries=queries, key_vectors=key_vectors, values=values, gate_log=gate_log, write_rate=write_rate, prompt_stretches=prompt_stretches, decode_owner=decode_owner, norm_gain=norm_gain, out_weight=out_weight)


HIGH = lax.Precision.HIGHEST

def unit_rows(vectors):
    return vectors * lax.rsqrt(lax.optimization_barrier(jnp.sum(vectors * vectors, axis=-1, keepdims=True)) + 1e-06)

def stretch_terms(query_part, key_part, value_part, gate_part, rate_part):
    length = gate_part.shape[-1]
    cumulative = jnp.cumsum(gate_part, axis=-1)
    row_index = lax.broadcasted_iota(jnp.int32, (length, length), 0)
    col_index = lax.broadcasted_iota(jnp.int32, (length, length), 1)
    spread = cumulative[:, :, None] - cumulative[:, None, :]
    strict = jnp.exp(jnp.where(row_index > col_index, spread, -jnp.inf))
    causal = jnp.exp(jnp.where(row_index >= col_index, spread, -jnp.inf))
    key_gram = jnp.einsum('hid,hjd->hij', key_part, key_part, precision=HIGH)
    system = jnp.eye(length, dtype=jnp.float32) + rate_part[:, :, None] * key_gram * strict
    growth = jnp.exp(cumulative)
    targets = jnp.concatenate([rate_part[:, :, None] * key_part * growth[:, :, None], rate_part[:, :, None] * value_part], axis=-1)
    solved = jax.scipy.linalg.solve_triangular(system, targets, lower=True, unit_diagonal=True)
    width = key_part.shape[-1]
    key_mix = solved[..., :width]
    fresh_base = solved[..., width:]
    scores = jnp.einsum('hid,hjd->hij', query_part, key_part, precision=HIGH) * causal
    query_decay = query_part * growth[:, :, None]
    key_decay = key_part * jnp.exp(cumulative[:, -1:] - cumulative)[:, :, None]
    retain = jnp.exp(cumulative[:, -1])
    return (key_mix, fresh_base, scores, query_decay, key_decay, retain)

def stretch_inputs(query_rows, key_rows, value_rows, gate_rows, rate_rows, repeat):
    length = query_rows.shape[0]
    query_part = unit_rows(query_rows.astype(jnp.float32).reshape(length, -1, DK)) * DK ** (-0.5)
    key_part = unit_rows(key_rows.astype(jnp.float32).reshape(length, -1, DK))
    query_part = jnp.repeat(query_part, repeat, axis=1).transpose(1, 0, 2)
    key_part = jnp.repeat(key_part, repeat, axis=1).transpose(1, 0, 2)
    value_part = value_rows.astype(jnp.float32).reshape(length, -1, DV).transpose(1, 0, 2)
    return stretch_terms(query_part, key_part, value_part, gate_rows, rate_rows)

def stretch_output(state, terms):
    key_mix, fresh_base, scores, query_decay, key_decay, retain = terms
    fresh = fresh_base - jnp.einsum('hcd,hde->hce', key_mix, state, precision=HIGH)
    output = jnp.einsum('hcd,hde->hce', query_decay, state, precision=HIGH) + jnp.einsum('hij,hje->hie', scores, fresh, precision=HIGH)
    following = retain[:, None, None] * state + jnp.einsum('hcd,hce->hde', key_decay, fresh, precision=HIGH)
    return (output, following)

def head_norm(output, norm_gain):
    scaled = output * lax.rsqrt(lax.optimization_barrier(jnp.mean(output * output, axis=-1, keepdims=True)) + 1e-06) * norm_gain
    return scaled.astype(jnp.bfloat16)

def prompt_layout(prompt_stretches, stretch_ids):
    finish = jnp.cumsum(prompt_stretches).astype(jnp.int32)
    begin = finish - prompt_stretches
    opens = jnp.any(stretch_ids[:, None] == begin[None, :], axis=1)
    closes = jnp.any(stretch_ids[:, None] + 1 == finish[None, :], axis=1)
    owner_prompt = lax.optimization_barrier(jnp.sum((finish[None, :] <= stretch_ids[:, None]).astype(jnp.int32), axis=1))
    return (finish, opens, closes, owner_prompt)

def reference(queries, key_vectors, values, gate_log, write_rate, prompt_stretches, decode_owner, norm_gain, out_weight):
    total = queries.shape[0]
    number = total // STRETCH
    repeat = VALUE_HEADS // HK
    stretch_ids = jnp.arange(number, dtype=jnp.int32)
    finish, opens, closes, owner_prompt = prompt_layout(prompt_stretches, stretch_ids)
    query_blocks = queries.reshape(number, STRETCH, -1)
    key_blocks = key_vectors.reshape(number, STRETCH, -1)
    value_blocks = values.reshape(number, STRETCH, -1)
    gate_blocks = gate_log.reshape(VALUE_HEADS, number, STRETCH).transpose(1, 0, 2)
    rate_blocks = write_rate.reshape(VALUE_HEADS, number, STRETCH).transpose(1, 0, 2)

    def advance(carry, inputs):
        state, table = carry
        query_rows, key_rows, value_rows, gate_rows, rate_rows, opening, closing, prompt = inputs
        terms = stretch_inputs(query_rows, key_rows, value_rows, gate_rows, rate_rows, repeat)
        state = jnp.where(opening, jnp.zeros_like(state), state)
        output, following = stretch_output(state, terms)
        prompt = jnp.minimum(prompt, PROMPTS - 1).astype(jnp.int32)
        current = lax.dynamic_index_in_dim(table, prompt, 0, keepdims=False)
        table = lax.dynamic_update_index_in_dim(table, jnp.where(closing, following, current), prompt, 0)
        return ((following, table), head_norm(output, norm_gain))
    start_state = jnp.zeros((VALUE_HEADS, DK, DV), jnp.float32)
    start_table = jnp.zeros((PROMPTS, VALUE_HEADS, DK, DV), jnp.float32)
    (final_state, table), normed = lax.scan(advance, (start_state, start_table), (query_blocks, key_blocks, value_blocks, gate_blocks, rate_blocks, opens, closes, owner_prompt))
    hidden = normed.transpose(0, 2, 1, 3).reshape(total, VALUE_HEADS * DV)
    group = VALUE_HEADS * DV // N_HEAD
    mixed = jnp.zeros((total, D_MODEL), jnp.float32)
    for index in range(N_HEAD):
        partial_sum = jnp.dot(hidden[:, index * group:(index + 1) * group].astype(jnp.float32), out_weight[index * group:(index + 1) * group].astype(jnp.float32), preferred_element_type=jnp.float32).astype(jnp.bfloat16)
        partial_sum = lax.optimization_barrier(partial_sum)
        mixed = mixed + partial_sum.astype(jnp.float32)
    decode_states = jnp.zeros((N_SEQ, VALUE_HEADS, DK, DV), jnp.float32).at[decode_owner].set(table)
    return (mixed.astype(jnp.bfloat16), decode_states)
```

```python
import functools

import jax
import jax.numpy as jnp
from jax import lax
from jax.experimental import pallas as pl
from jax.experimental.pallas import tpu as pltpu
from jax.sharding import PartitionSpec as P

DK = 128
DV = 128
STRETCH = 64
PAIR = 2 * STRETCH
BF = jnp.bfloat16
F32 = jnp.float32
HIGH = lax.Precision.HIGHEST


def mm(a, b):
    return jnp.dot(a, b, preferred_element_type=F32)


def mm_t(a, b):
    return lax.dot_general(a, b, (((1,), (1,)), ((), ())), preferred_element_type=F32)


def split(x):
    high = x.astype(BF)
    return high, (x - high.astype(F32)).astype(BF)


def local_kernel(
    repeat, prompts, ps_ref, q_ref, k_ref, v_ref, gate_ref, rate_ref,
    o_ref, y_ref, l_ref, m_ref, cl_ref, cm_ref,
):
    h = pl.program_id(0)
    rows = q_ref.shape[0]
    number = rows // STRETCH
    blocks = rows // PAIR
    base = lax.axis_index("seq") * number
    ri = lax.broadcasted_iota(jnp.int32, (PAIR, PAIR), 0)
    ci = lax.broadcasted_iota(jnp.int32, (PAIR, PAIR), 1)
    same = (ri // STRETCH) == (ci // STRETCH)
    eye = ri == ci
    strict_mask = same & (ri > ci)
    causal_mask = same & (ri >= ci)
    eye_f = eye.astype(F32)
    eye_b = eye_f.astype(BF)
    upto = (same & (ri <= ci)).astype(F32)
    after = (same & (ri > ci)).astype(F32)
    first_half = lax.broadcasted_iota(jnp.int32, (PAIR, 1), 0) < STRETCH

    gram, scores0, keys, keys_t, qs, qscale = [], [], [], [], [], []
    rk_row, rk_col = [], []
    for c in range(blocks):
        sl = slice(c * PAIR, (c + 1) * PAIR)
        k = k_ref[sl, :]
        q = q_ref[sl, :]
        g = mm_t(k, k)
        s = mm_t(q, k)
        gram.append(g)
        scores0.append(s)
        keys.append(k)
        keys_t.append(k.T)
        diag = jnp.where(eye, g, 0.0)
        rk_row.append(lax.rsqrt(jnp.sum(diag, axis=0, keepdims=True) + 1e-06))
        rk_col.append(lax.rsqrt(jnp.sum(diag, axis=1, keepdims=True) + 1e-06))
        qf = q.astype(F32)
        qs.append(qf)
        qscale.append(lax.rsqrt(jnp.sum(qf * qf, axis=1, keepdims=True) + 1e-06) * DK ** (-0.5))

    grow_all, suf_all = [], []
    for c in range(blocks):
        gate = gate_ref[:, c * PAIR:(c + 1) * PAIR]
        grow_all.append(jnp.dot(gate, upto, preferred_element_type=F32, precision=HIGH))
        suf_all.append(jnp.dot(gate, after, preferred_element_type=F32, precision=HIGH))
    head_row = lax.broadcasted_iota(jnp.int32, (gate_ref.shape[0], PAIR), 0)
    items = [(c, r) for r in range(repeat) for c in range(blocks)]
    lower, inv, info = [], [], []
    for c, r in items:
        sl = slice(c * PAIR, (c + 1) * PAIR)
        pick = head_row == h * repeat + r
        grow, suf, rate = [
            jnp.sum(jnp.where(pick, x, 0.0), axis=0, keepdims=True)
            for x in (grow_all[c], suf_all[c], rate_ref[:, sl])
        ]
        stack = jnp.concatenate([grow, suf, rate, jnp.zeros((5, PAIR), F32)], axis=0)
        cols = stack.T
        gcol, sufcol, bcol = cols[:, 0:1], cols[:, 1:2], cols[:, 2:3]
        decay = jnp.exp(jnp.where(causal_mask, gcol - grow, -jnp.inf))
        a = jnp.where(strict_mask, (bcol * rk_col[c]) * gram[c] * rk_row[c] * decay, 0.0)
        sc = scores0[c] * (qscale[c] * rk_row[c]) * decay
        lower.append(a)
        inv.append(jnp.where(eye, 1.0, jnp.where((ri // 2) == (ci // 2), -a, 0.0)))
        info.append((grow, rate, gcol, sufcol, sc))

    size = 2
    while size < STRETCH:
        off = ((ri // (2 * size)) == (ci // (2 * size))) & ((ri // size) != (ci // size))
        invb = [t.astype(BF) for t in inv]
        part = [
            mm(jnp.where(off, a, 0.0).astype(BF), tb).astype(BF) for a, tb in zip(lower, invb)
        ]
        inv = [t - mm(tb, p) for t, tb, p in zip(inv, invb, part)]
        size *= 2

    solved = []
    invb = [t.astype(BF) for t in inv]
    resid = []
    for a, tb in zip(lower, invb):
        hi, lo = split(a)
        resid.append((eye_f - tb.astype(F32)) - (mm(hi, tb) + mm(lo, tb)))
    inv = [tb.astype(F32) + mm(tb, e.astype(BF)) for tb, e in zip(invb, resid)]
    wu = []
    for (c, r), t, (grow, rate, gcol, sufcol, sc) in zip(items, inv, info):
        sl = slice(c * PAIR, (c + 1) * PAIR)
        v = v_ref[sl, r * DV:(r + 1) * DV]
        wh, wl = split(t * (rate * jnp.exp(grow) * rk_row[c]))
        uh, ul = split(t * rate)
        w = mm(wh, keys[c]) + mm(wl, keys[c])
        u = mm(uh, v) + mm(ul, v)
        wu.append((w, u))
    trans, qside = [], []
    for (c, r), (w, u), (grow, rate, gcol, sufcol, sc) in zip(items, wu, info):
        both = jnp.concatenate([w, u], axis=1)
        d = jnp.exp(sufcol) * rk_col[c]
        scaled = both * d
        t0 = mm(keys_t[c], jnp.where(first_half, scaled, 0.0).astype(BF))
        t1 = mm(keys_t[c], jnp.where(first_half, 0.0, scaled).astype(BF))
        sw = mm(sc.astype(BF), both.astype(BF))
        qe = qs[c] * (qscale[c] * jnp.exp(gcol)) - sw[:, :DK]
        trans.append((t0, t1))
        qside.append((qe.astype(BF), sw[:, DK:]))

    finish = []
    begin = []
    total = jnp.int32(0)
    for p in range(prompts):
        begin.append(total)
        total = total + ps_ref[p]
        finish.append(total)

    cl_ref[...] = jnp.zeros_like(cl_ref)
    cm_ref[...] = jnp.zeros_like(cm_ref)
    zero = jnp.zeros((DK, DV), F32)
    states = [jnp.concatenate([zero, eye_f], axis=1) for _ in range(repeat)]
    for n in range(number):
        c, half = n // 2, n % 2
        opens = begin[0] == base + n
        for p in range(1, prompts):
            opens = opens | (begin[p] == base + n)
        closing = jnp.int32(-1)
        for p in range(prompts):
            closing = jnp.where(finish[p] == base + n + 1, jnp.int32(p), closing)
        keep = jnp.where(opens, 0.0, 1.0).astype(F32)
        following = []
        for r in range(repeat):
            i = r * blocks + c
            x = states[r] * keep
            xb = x.astype(BF)
            hs = slice(half * STRETCH, (half + 1) * STRETCH)
            rs = slice(n * STRETCH, (n + 1) * STRETCH)
            qe, su = qside[i]
            oy = mm(qe[hs], xb)
            cs = slice(r * DV, (r + 1) * DV)
            o_ref[rs, cs] = oy[:, :DV] + su[hs]
            y_ref[rs, cs] = oy[:, DV:].astype(BF)
            t = trans[i][half]
            last = (half + 1) * STRETCH - 1
            retain = jnp.exp(info[i][0][:, last:last + 1])
            moved = retain * x - mm(t[:, :DK].astype(BF), xb)
            following.append(
                jnp.concatenate([moved[:, :DV] + t[:, DK:], moved[:, DV:]], axis=1)
            )
        states = following

        @pl.when(closing >= 0)
        def _(following=following, closing=closing):
            for r in range(repeat):
                cl_ref[closing, r] = following[r][:, :DV]
                cm_ref[closing, r] = following[r][:, DV:].astype(BF)

    for r in range(repeat):
        l_ref[r] = states[r][:, :DV]
        m_ref[r] = states[r][:, DV:].astype(BF)


def local_part(queries, key_vectors, values, gate_log, write_rate, prompt_stretches):
    rows = queries.shape[0]
    heads = gate_log.shape[0]
    groups = queries.shape[1] // DK
    repeat = heads // groups
    prompts = prompt_stretches.shape[0]
    whole = pl.BlockSpec((heads, rows), lambda h: (0, 0))
    wide = pl.BlockSpec((rows, repeat * DV), lambda h: (0, h))
    return pl.pallas_call(
        functools.partial(local_kernel, repeat, prompts),
        grid=(groups,),
        in_specs=[
            pl.BlockSpec(memory_space=pltpu.SMEM),
            pl.BlockSpec((rows, DK), lambda h: (0, h)),
            pl.BlockSpec((rows, DK), lambda h: (0, h)),
            wide,
            whole,
            whole,
        ],
        out_specs=[
            wide,
            wide,
            pl.BlockSpec((repeat, DK, DV), lambda h: (h, 0, 0)),
            pl.BlockSpec((repeat, DK, DK), lambda h: (h, 0, 0)),
            pl.BlockSpec((prompts, repeat, DK, DV), lambda h: (0, h, 0, 0)),
            pl.BlockSpec((prompts, repeat, DK, DK), lambda h: (0, h, 0, 0)),
        ],
        out_shape=[
            jax.ShapeDtypeStruct((rows, heads * DV), F32),
            jax.ShapeDtypeStruct((rows, heads * DV), BF),
            jax.ShapeDtypeStruct((heads, DK, DV), F32),
            jax.ShapeDtypeStruct((heads, DK, DK), BF),
            jax.ShapeDtypeStruct((prompts, heads, DK, DV), F32),
            jax.ShapeDtypeStruct((prompts, heads, DK, DK), BF),
        ],
        compiler_params=pltpu.CompilerParams(vmem_limit_bytes=48 * 1024 * 1024),
    )(prompt_stretches, queries, key_vectors, values, gate_log, write_rate)


def finish_kernel(heads, o_ref, y_ref, inc_ref, cl_ref, cm_ref, gain_ref, w_ref, part_ref, table_ref, hid):
    step = pl.program_id(0)

    @pl.when(step == 0)
    def _():
        gain = gain_ref[...]
        for j in range(heads):
            cs = slice(j * DV, (j + 1) * DV)
            out = o_ref[:, cs] + mm(y_ref[:, cs], inc_ref[j])
            mean = jnp.mean(out * out, axis=1, keepdims=True)
            hid[:, cs] = (out * lax.rsqrt(mean + 1e-06) * gain).astype(BF)

    for j in range(heads):
        table_ref[0, j] = (cl_ref[0, j] + mm(cm_ref[0, j], inc_ref[j])).astype(BF)
    part_ref[0] = mm(hid[...], w_ref[...]).astype(BF)


def finish_part(o_loc, y_map, incoming, close_l, close_m, norm_gain, out_weight, parts):
    rows, width = o_loc.shape
    heads = width // DV
    prompts = close_l.shape[0]
    assert prompts <= parts
    cols = out_weight.shape[1] // parts
    full = pl.BlockSpec((rows, width), lambda s: (0, 0))
    return pl.pallas_call(
        functools.partial(finish_kernel, heads),
        grid=(parts,),
        in_specs=[
            full,
            full,
            pl.BlockSpec((heads, DK, DV), lambda s: (0, 0, 0)),
            pl.BlockSpec((1, heads, DK, DV), lambda s: (jnp.minimum(s, prompts - 1), 0, 0, 0)),
            pl.BlockSpec((1, heads, DK, DK), lambda s: (jnp.minimum(s, prompts - 1), 0, 0, 0)),
            pl.BlockSpec((1, DV), lambda s: (0, 0)),
            pl.BlockSpec((width, cols), lambda s: (0, s)),
        ],
        out_specs=[
            pl.BlockSpec((1, rows, cols), lambda s: (s, 0, 0)),
            pl.BlockSpec((1, heads, DK, DV), lambda s: (jnp.minimum(s, prompts - 1), 0, 0, 0)),
        ],
        out_shape=[
            jax.ShapeDtypeStruct((parts, rows, cols), BF),
            jax.ShapeDtypeStruct((prompts, heads, DK, DV), BF),
        ],
        scratch_shapes=[pltpu.VMEM((rows, width), BF)],
        compiler_params=pltpu.CompilerParams(vmem_limit_bytes=48 * 1024 * 1024),
    )(o_loc, y_map, incoming, close_l, close_m, norm_gain.reshape(1, -1), out_weight)


def relay(local_state, local_map, devices_seq):
    route = [(i, i + 1) for i in range(devices_seq - 1)]
    incoming = lax.ppermute(local_state.astype(BF), "seq", route)
    for _ in range(devices_seq // 2 - 1):
        outgoing = jnp.einsum("hde,hef->hdf", local_map, incoming, preferred_element_type=F32)
        incoming = lax.ppermute((outgoing + local_state).astype(BF), "seq", route)
    return incoming


def body(
    queries, key_vectors, values, gate_log, write_rate,
    prompt_stretches, decode_owner, norm_gain, out_weight,
):
    position = lax.axis_index("seq")
    devices_seq = lax.axis_size("seq")
    o_loc, y_map, local_state, local_map, close_l, close_m = local_part(
        queries, key_vectors, values, gate_log, write_rate, prompt_stretches
    )
    incoming = relay(local_state, local_map, devices_seq)
    parts = lax.axis_size("head")
    partial_sum, table = finish_part(
        o_loc, y_map, incoming, close_l, close_m, norm_gain, out_weight, parts
    )
    table = lax.psum(table, "seq")
    mine = (decode_owner == position).astype(F32)
    owned = jnp.sum(table.astype(F32) * mine[:, None, None, None], axis=0)
    mixed = lax.psum_scatter(partial_sum, "head", scatter_dimension=0, tiled=True)
    return (mixed[0], owned[None])


def solution(mesh):
    return jax.shard_map(
        body,
        mesh=mesh,
        in_specs=(
            P("seq", "head"),
            P("seq", "head"),
            P("seq", "head"),
            P("head", "seq"),
            P("head", "seq"),
            P(),
            P(),
            P(),
            P("head", None),
        ),
        out_specs=(P("seq", "head"), P("seq", "head", None, None)),
        check_vma=False,
    )
```

```python
import functools

import jax
import jax.numpy as jnp
from jax import lax
from jax.experimental import pallas as pl
from jax.experimental.pallas import tpu as pltpu
from jax.sharding import PartitionSpec as P

DK = 128
DV = 128
STRETCH = 64
PAIR = 2 * STRETCH
BF = jnp.bfloat16
F32 = jnp.float32
HIGH = lax.Precision.HIGHEST


def mm(a, b):
    return jnp.dot(a, b, preferred_element_type=F32)


def mm_t(a, b):
    return lax.dot_general(a, b, (((1,), (1,)), ((), ())), preferred_element_type=F32)


def split(x):
    high = x.astype(BF)
    return high, (x - high.astype(F32)).astype(BF)


def local_kernel(
    repeat, prompts, ps_ref, q_ref, k_ref, v_ref, gate_ref, rate_ref,
    o_ref, y_ref, l_ref, m_ref, cl_ref, cm_ref,
):
    h = pl.program_id(0)
    rows = q_ref.shape[0]
    number = rows // STRETCH
    blocks = rows // PAIR
    base = lax.axis_index("seq") * number
    ri = lax.broadcasted_iota(jnp.int32, (PAIR, PAIR), 0)
    ci = lax.broadcasted_iota(jnp.int32, (PAIR, PAIR), 1)
    same = (ri // STRETCH) == (ci // STRETCH)
    eye = ri == ci
    strict_mask = same & (ri > ci)
    causal_mask = same & (ri >= ci)
    eye_f = eye.astype(F32)
    eye_b = eye_f.astype(BF)
    upto = (same & (ri <= ci)).astype(F32)
    after = (same & (ri > ci)).astype(F32)
    first_half = lax.broadcasted_iota(jnp.int32, (PAIR, 1), 0) < STRETCH

    gram, scores0, keys, keys_t, qs, qscale = [], [], [], [], [], []
    rk_row, rk_col = [], []
    for c in range(blocks):
        sl = slice(c * PAIR, (c + 1) * PAIR)
        k = k_ref[sl, :]
        q = q_ref[sl, :]
        g = mm_t(k, k)
        s = mm_t(q, k)
        gram.append(g)
        scores0.append(s)
        keys.append(k)
        keys_t.append(k.T)
        diag = jnp.where(eye, g, 0.0)
        rk_row.append(lax.rsqrt(jnp.sum(diag, axis=0, keepdims=True) + 1e-06))
        rk_col.append(lax.rsqrt(jnp.sum(diag, axis=1, keepdims=True) + 1e-06))
        qf = q.astype(F32)
        qs.append(qf)
        qscale.append(lax.rsqrt(jnp.sum(qf * qf, axis=1, keepdims=True) + 1e-06) * DK ** (-0.5))

    grow_all, suf_all = [], []
    for c in range(blocks):
        gate = gate_ref[:, c * PAIR:(c + 1) * PAIR]
        grow_all.append(jnp.dot(gate, upto, preferred_element_type=F32, precision=HIGH))
        suf_all.append(jnp.dot(gate, after, preferred_element_type=F32, precision=HIGH))
    head_row = lax.broadcasted_iota(jnp.int32, (gate_ref.shape[0], PAIR), 0)
    items = [(c, r) for r in range(repeat) for c in range(blocks)]
    lower, inv, info = [], [], []
    for c, r in items:
        sl = slice(c * PAIR, (c + 1) * PAIR)
        pick = head_row == h * repeat + r
        grow, suf, rate = [
            jnp.sum(jnp.where(pick, x, 0.0), axis=0, keepdims=True)
            for x in (grow_all[c], suf_all[c], rate_ref[:, sl])
        ]
        stack = jnp.concatenate([grow, suf, rate, jnp.zeros((5, PAIR), F32)], axis=0)
        cols = stack.T
        gcol, sufcol, bcol = cols[:, 0:1], cols[:, 1:2], cols[:, 2:3]
        decay = jnp.exp(jnp.where(causal_mask, gcol - grow, -jnp.inf))
        a = jnp.where(strict_mask, (bcol * rk_col[c]) * gram[c] * rk_row[c] * decay, 0.0)
        sc = scores0[c] * (qscale[c] * rk_row[c]) * decay
        lower.append(a)
        inv.append(jnp.where(eye, 1.0, jnp.where((ri // 2) == (ci // 2), -a, 0.0)))
        info.append((grow, rate, gcol, sufcol, sc))

    size = 2
    while size < STRETCH:
        off = ((ri // (2 * size)) == (ci // (2 * size))) & ((ri // size) != (ci // size))
        invb = [t.astype(BF) for t in inv]
        part = [
            mm(jnp.where(off, a, 0.0).astype(BF), tb).astype(BF) for a, tb in zip(lower, invb)
        ]
        inv = [t - mm(tb, p) for t, tb, p in zip(inv, invb, part)]
        size *= 2

    solved = []
    invb = [t.astype(BF) for t in inv]
    resid = []
    for a, tb in zip(lower, invb):
        hi, lo = split(a)
        resid.append((eye_f - tb.astype(F32)) - (mm(hi, tb) + mm(lo, tb)))
    inv = [tb.astype(F32) + mm(tb, e.astype(BF)) for tb, e in zip(invb, resid)]
    wu = []
    for (c, r), t, (grow, rate, gcol, sufcol, sc) in zip(items, inv, info):
        sl = slice(c * PAIR, (c + 1) * PAIR)
        v = v_ref[sl, r * DV:(r + 1) * DV]
        wh, wl = split(t * (rate * jnp.exp(grow) * rk_row[c]))
        uh, ul = split(t * rate)
        w = mm(wh, keys[c]) + mm(wl, keys[c])
        u = mm(uh, v) + mm(ul, v)
        wu.append((w, u))
    trans, qside = [], []
    for (c, r), (w, u), (grow, rate, gcol, sufcol, sc) in zip(items, wu, info):
        both = jnp.concatenate([w, u], axis=1)
        d = jnp.exp(sufcol) * rk_col[c]
        scaled = both * d
        t0 = mm(keys_t[c], jnp.where(first_half, scaled, 0.0).astype(BF))
        t1 = mm(keys_t[c], jnp.where(first_half, 0.0, scaled).astype(BF))
        sw = mm(sc.astype(BF), both.astype(BF))
        qe = qs[c] * (qscale[c] * jnp.exp(gcol)) - sw[:, :DK]
        trans.append((t0, t1))
        qside.append((qe.astype(BF), sw[:, DK:]))

    finish = []
    begin = []
    total = jnp.int32(0)
    for p in range(prompts):
        begin.append(total)
        total = total + ps_ref[p]
        finish.append(total)

    cl_ref[...] = jnp.zeros_like(cl_ref)
    cm_ref[...] = jnp.zeros_like(cm_ref)
    zero = jnp.zeros((DK, DV), F32)
    states = [jnp.concatenate([zero, eye_f], axis=1) for _ in range(repeat)]
    for n in range(number):
        c, half = n // 2, n % 2
        opens = begin[0] == base + n
        for p in range(1, prompts):
            opens = opens | (begin[p] == base + n)
        closing = jnp.int32(-1)
        for p in range(prompts):
            closing = jnp.where(finish[p] == base + n + 1, jnp.int32(p), closing)
        keep = jnp.where(opens, 0.0, 1.0).astype(F32)
        following = []
        for r in range(repeat):
            i = r * blocks + c
            x = states[r] * keep
            xb = x.astype(BF)
            hs = slice(half * STRETCH, (half + 1) * STRETCH)
            rs = slice(n * STRETCH, (n + 1) * STRETCH)
            qe, su = qside[i]
            oy = mm(qe[hs], xb)
            cs = slice(r * DV, (r + 1) * DV)
            o_ref[rs, cs] = oy[:, :DV] + su[hs]
            y_ref[rs, cs] = oy[:, DV:].astype(BF)
            t = trans[i][half]
            last = (half + 1) * STRETCH - 1
            retain = jnp.exp(info[i][0][:, last:last + 1])
            moved = retain * x - mm(t[:, :DK].astype(BF), xb)
            following.append(
                jnp.concatenate([moved[:, :DV] + t[:, DK:], moved[:, DV:]], axis=1)
            )
        states = following

        @pl.when(closing >= 0)
        def _(following=following, closing=closing):
            for r in range(repeat):
                cl_ref[closing, r] = following[r][:, :DV]
                cm_ref[closing, r] = following[r][:, DV:].astype(BF)

    for r in range(repeat):
        l_ref[r] = states[r][:, :DV]
        m_ref[r] = states[r][:, DV:].astype(BF)


def local_part(queries, key_vectors, values, gate_log, write_rate, prompt_stretches):
    rows = queries.shape[0]
    heads = gate_log.shape[0]
    groups = queries.shape[1] // DK
    repeat = heads // groups
    prompts = prompt_stretches.shape[0]
    whole = pl.BlockSpec((heads, rows), lambda h: (0, 0))
    wide = pl.BlockSpec((rows, repeat * DV), lambda h: (0, h))
    return pl.pallas_call(
        functools.partial(local_kernel, repeat, prompts),
        grid=(groups,),
        in_specs=[
            pl.BlockSpec(memory_space=pltpu.SMEM),
            pl.BlockSpec((rows, DK), lambda h: (0, h)),
            pl.BlockSpec((rows, DK), lambda h: (0, h)),
            wide,
            whole,
            whole,
        ],
        out_specs=[
            wide,
            wide,
            pl.BlockSpec((repeat, DK, DV), lambda h: (h, 0, 0)),
            pl.BlockSpec((repeat, DK, DK), lambda h: (h, 0, 0)),
            pl.BlockSpec((prompts, repeat, DK, DV), lambda h: (0, h, 0, 0)),
            pl.BlockSpec((prompts, repeat, DK, DK), lambda h: (0, h, 0, 0)),
        ],
        out_shape=[
            jax.ShapeDtypeStruct((rows, heads * DV), F32),
            jax.ShapeDtypeStruct((rows, heads * DV), BF),
            jax.ShapeDtypeStruct((heads, DK, DV), F32),
            jax.ShapeDtypeStruct((heads, DK, DK), BF),
            jax.ShapeDtypeStruct((prompts, heads, DK, DV), F32),
            jax.ShapeDtypeStruct((prompts, heads, DK, DK), BF),
        ],
        compiler_params=pltpu.CompilerParams(vmem_limit_bytes=48 * 1024 * 1024),
    )(prompt_stretches, queries, key_vectors, values, gate_log, write_rate)


def tail_kernel(
    heads, prompts, devices, groups,
    l_ref, m_ref, mask_ref, gain_ref, o_hbm, y_hbm, cl_hbm, cm_hbm, w_hbm,
    mixed_ref, owned_ref,
    o_ref, y_ref, cl_ref, cm_ref, w_ref, inc, nxt, pair_out, pair_in, own,
    up_in, up_out, down_in, down_out, sel_out, sel_in, hid, core_out, core_in, x_out, x_in,
    load_sem, chain_s, chain_r, pair_s, pair_r, up_s, up_r, down_s, down_r,
    sel_s, sel_r, core_s, core_r, x_s, x_r,
):
    pos = lax.axis_index("seq")
    head = lax.axis_index("head")
    half = prompts // 2
    xs = groups // 2
    here, core = head // 2, lax.rem(head, 2)
    side = lax.rem(pos, 2)
    mate = pos + 1 - 2 * side
    right, left = lax.rem(pos + 1, devices), lax.rem(pos + devices - 1, devices)
    above, below = lax.rem(pos + 2, devices), lax.rem(pos + devices - 2, devices)
    cols = w_ref.shape[1] // groups

    loads = [
        pltpu.make_async_copy(src, dst, load_sem.at[i])
        for i, (src, dst) in enumerate(
            [(cl_hbm, cl_ref), (cm_hbm, cm_ref), (o_hbm, o_ref), (y_hbm, y_ref), (w_hbm, w_ref)]
        )
    ]
    for load in loads:
        load.start()

    barrier = pltpu.get_barrier_semaphore()
    has_left, has_right = pos >= 1, pos <= devices - 2
    has_below, has_above = pos >= 2, pos <= devices - 3
    count = jnp.int32(xs)
    for has, other in (
        (has_left, left), (has_right, right), (has_below, below), (has_above, above)
    ):
        count = count + has.astype(jnp.int32)

        @pl.when(has)
        def _(other=other):
            pl.semaphore_signal(
                barrier, inc=1, device_id={"seq": other}, device_id_type=pl.DeviceIdType.MESH
            )
    x_heads = [lax.rem(here + k, xs) * 2 + core for k in range(1, xs)]
    for other in [here * 2 + 1 - core] + x_heads:
        pl.semaphore_signal(
            barrier, inc=1, device_id={"head": other}, device_id_type=pl.DeviceIdType.MESH
        )
    pl.semaphore_wait(barrier, count)

    def remote(src, dst, send, recv, **where):
        return pltpu.make_async_remote_copy(
            src_ref=src, dst_ref=dst, send_sem=send, recv_sem=recv,
            device_id=where, device_id_type=pl.DeviceIdType.MESH,
        )

    def chain(h):
        return remote(nxt.at[h], inc.at[h], chain_s.at[h], chain_r.at[h], seq=right)

    def pair(h):
        return remote(pair_out.at[h], pair_in.at[h], pair_s.at[h], pair_r.at[h], seq=mate)

    def upward(h):
        return remote(up_out.at[h], up_in.at[h], up_s.at[h], up_r.at[h], seq=above)

    def downward(h):
        return remote(down_out.at[h], down_in.at[h], down_s.at[h], down_r.at[h], seq=below)

    def deliver(h):
        return remote(sel_out.at[h], sel_in.at[h], sel_s.at[h], sel_r.at[h], seq=mate)

    def to_core(k):
        return remote(
            core_out.at[k], core_in.at[k], core_s.at[k], core_r.at[k], head=here * 2 + 1 - core
        )

    def to_x(k):
        return remote(
            x_out.at[k - 1], x_in.at[k - 1], x_s.at[k - 1], x_r.at[k - 1], head=x_heads[k - 1]
        )

    @pl.when(pos == 0)
    def _():
        inc[...] = jnp.zeros_like(inc)

    def chain_step(h, _):
        @pl.when(has_left)
        def _():
            chain(h).wait_recv()

        nxt[h] = (mm(m_ref[h], inc[h]) + l_ref[h]).astype(BF)

        @pl.when(has_right)
        def _():
            chain(h).start()

        return 0

    lax.fori_loop(0, heads, chain_step, 0)

    loads[0].wait()
    loads[1].wait()

    def table(p, h):
        return (cl_ref[p, h] + mm(cm_ref[p, h], inc[h])).astype(BF)

    def pair_step(h, _):
        for i in range(half):
            pair_out[h, i] = table((1 - side) * half + i, h)
        pair(h).start()
        for i in range(half):
            own[h, i] = table(side * half + i, h)
        return 0

    lax.fori_loop(0, heads, pair_step, 0)

    loads[2].wait()
    loads[3].wait()
    gain = gain_ref[...]
    for j in range(heads):
        cs = slice(j * DV, (j + 1) * DV)
        out = o_ref[:, cs] + mm(y_ref[:, cs], inc[j])
        mean = jnp.mean(out * out, axis=1, keepdims=True)
        hid[:, cs] = (out * lax.rsqrt(mean + 1e-06) * gain).astype(BF)
    loads[4].wait()

    def project(k, which):
        slot = lax.rem(here + k, xs) * 2 + which
        w = w_ref[:, pl.ds(pl.multiple_of(slot * cols, 128), cols)]
        return mm(hid[...], w)

    order = list(range(1, xs)) + [0]
    for k in order:
        core_out[k] = project(k, 1 - core).astype(BF)
        to_core(k).start()
    for k in range(1, xs):
        mine = project(k, core)
        to_core(k).wait_recv()
        x_out[k - 1] = (mine + core_in[k].astype(F32)).astype(BF)
        to_x(k).start()

    def gather_step(h, _):
        pair(h).wait_recv()
        own[h] = own[h] + pair_in[h]
        return 0

    lax.fori_loop(0, heads, gather_step, 0)

    @pl.when(pos < 2)
    def _():
        up_in[...] = jnp.zeros_like(up_in)

    @pl.when(pos >= devices - 2)
    def _():
        down_in[...] = jnp.zeros_like(down_in)

    def up_step(h, _):
        @pl.when(has_below)
        def _():
            upward(h).wait_recv()

        @pl.when(has_above)
        def _():
            up_out[h] = up_in[h] + own[h]
            upward(h).start()

        return 0

    def down_step(h, _):
        @pl.when(has_above)
        def _():
            downward(h).wait_recv()

        @pl.when(has_below)
        def _():
            down_out[h] = down_in[h] + own[h]
            downward(h).start()

        return 0

    low = pos < devices // 2

    @pl.when(low)
    def _():
        lax.fori_loop(0, heads, up_step, 0)
        lax.fori_loop(0, heads, down_step, 0)

    @pl.when(jnp.logical_not(low))
    def _():
        lax.fori_loop(0, heads, down_step, 0)
        lax.fori_loop(0, heads, up_step, 0)

    def select_step(h, _):
        kept = jnp.zeros((DK, DV), F32)
        sent = jnp.zeros((DK, DV), F32)
        for i in range(half):
            full = (up_in[h, i] + own[h, i] + down_in[h, i]).astype(F32)
            p = side * half + i
            kept = kept + full * mask_ref[p]
            sent = sent + full * mask_ref[prompts + p]
        sel_out[h] = sent.astype(BF)
        deliver(h).start()
        owned_ref[0, h] = kept
        return 0

    lax.fori_loop(0, heads, select_step, 0)

    mine = project(0, core)
    to_core(0).wait_recv()
    total = mine + core_in[0].astype(F32)
    for k in range(1, xs):
        to_x(k).wait_recv()
        total = total + x_in[k - 1].astype(F32)
    mixed_ref[...] = total.astype(BF)

    def last_step(h, _):
        deliver(h).wait_recv()
        owned_ref[0, h] = owned_ref[0, h] + sel_in[h].astype(F32)
        pair(h).wait_send()
        deliver(h).wait_send()

        @pl.when(has_right)
        def _():
            chain(h).wait_send()

        @pl.when(has_above)
        def _():
            upward(h).wait_send()

        @pl.when(has_below)
        def _():
            downward(h).wait_send()

        return 0

    lax.fori_loop(0, heads, last_step, 0)
    for k in range(xs):
        to_core(k).wait_send()
    for k in range(1, xs):
        to_x(k).wait_send()


def tail_part(local_state, local_map, masks, norm_gain, o_loc, y_map, close_l, close_m, out_weight):
    rows, width = o_loc.shape
    heads = width // DV
    prompts = close_l.shape[0]
    half = prompts // 2
    devices = lax.axis_size("seq")
    groups = lax.axis_size("head")
    xs = groups // 2
    cols = out_weight.shape[1] // groups
    vmem = pl.BlockSpec(memory_space=pltpu.VMEM)
    anywhere = pl.BlockSpec(memory_space=pl.ANY)
    dma = pltpu.SemaphoreType.DMA
    line = pltpu.VMEM((heads, half, DK, DV), BF)
    state = pltpu.VMEM((heads, DK, DV), BF)
    return pl.pallas_call(
        functools.partial(tail_kernel, heads, prompts, devices, groups),
        in_specs=[vmem] * 4 + [anywhere] * 5,
        out_specs=[vmem, vmem],
        out_shape=[
            jax.ShapeDtypeStruct((rows, cols), BF),
            jax.ShapeDtypeStruct((1, heads, DK, DV), F32),
        ],
        scratch_shapes=[
            pltpu.VMEM(o_loc.shape, F32),
            pltpu.VMEM(y_map.shape, BF),
            pltpu.VMEM(close_l.shape, F32),
            pltpu.VMEM(close_m.shape, BF),
            pltpu.VMEM(out_weight.shape, BF),
            state, state, line, line, line, line, line, line, line, state, state,
            pltpu.VMEM((rows, width), BF),
            pltpu.VMEM((xs, rows, cols), BF),
            pltpu.VMEM((xs, rows, cols), BF),
            pltpu.VMEM((xs - 1, rows, cols), BF),
            pltpu.VMEM((xs - 1, rows, cols), BF),
            dma((5,)),
        ] + [dma((heads,))] * 10 + [dma((xs,))] * 2 + [dma((xs - 1,))] * 2,
        compiler_params=pltpu.CompilerParams(
            collective_id=0, has_side_effects=True, vmem_limit_bytes=48 * 1024 * 1024
        ),
    )(
        local_state, local_map, masks, norm_gain.reshape(1, -1),
        o_loc, y_map, close_l, close_m, out_weight,
    )


def body(
    queries, key_vectors, values, gate_log, write_rate,
    prompt_stretches, decode_owner, norm_gain, out_weight,
):
    position = lax.axis_index("seq")
    o_loc, y_map, local_state, local_map, close_l, close_m = local_part(
        queries, key_vectors, values, gate_log, write_rate, prompt_stretches
    )
    mate = position + 1 - 2 * (position % 2)
    masks = jnp.concatenate([decode_owner == position, decode_owner == mate]).astype(F32)
    masks = jnp.broadcast_to(masks[:, None, None], (masks.shape[0], 1, DV))
    return tail_part(
        local_state, local_map, masks, norm_gain, o_loc, y_map, close_l, close_m, out_weight
    )


def solution(mesh):
    return jax.shard_map(
        body,
        mesh=mesh,
        in_specs=(
            P("seq", "head"),
            P("seq", "head"),
            P("seq", "head"),
            P("head", "seq"),
            P("head", "seq"),
            P(),
            P(),
            P(),
            P("head", None),
        ),
        out_specs=(P("seq", "head"), P("seq", "head", None, None)),
        check_vma=False,
    )
```

```python
import functools

import jax
import jax.numpy as jnp
from jax import lax
from jax.experimental import pallas as pl
from jax.experimental.pallas import tpu as pltpu
from jax.sharding import PartitionSpec as P

DK = 128
DV = 128
STRETCH = 64
PAIR = 2 * STRETCH
BF = jnp.bfloat16
F32 = jnp.float32
HIGH = lax.Precision.HIGHEST


def mm(a, b):
    return jnp.dot(a, b, preferred_element_type=F32)


def mm_t(a, b):
    return lax.dot_general(a, b, (((1,), (1,)), ((), ())), preferred_element_type=F32)


def split(x):
    high = x.astype(BF)
    return high, (x - high.astype(F32)).astype(BF)


def local_kernel(
    repeat, prompts, ps_ref, owner_ref, q_ref, k_ref, v_ref, gate_ref, rate_ref,
    o_ref, y_ref, l_ref, m_ref, cl_ref, cm_ref, mask_ref,
):
    h = pl.program_id(0)
    rows = q_ref.shape[0]
    number = rows // STRETCH
    blocks = rows // PAIR
    position = lax.axis_index("seq")
    base = position * number
    mate = position + 1 - 2 * lax.rem(position, 2)
    for p in range(prompts):
        for i, place in enumerate((position, mate)):
            owned = jnp.where(owner_ref[p] == place, 1.0, 0.0).astype(F32)
            mask_ref[i * prompts + p] = jnp.full((1, DV), owned, F32)
    ri = lax.broadcasted_iota(jnp.int32, (PAIR, PAIR), 0)
    ci = lax.broadcasted_iota(jnp.int32, (PAIR, PAIR), 1)
    same = (ri // STRETCH) == (ci // STRETCH)
    eye = ri == ci
    strict_mask = same & (ri > ci)
    causal_mask = same & (ri >= ci)
    eye_f = eye.astype(F32)
    eye_b = eye_f.astype(BF)
    upto = (same & (ri <= ci)).astype(F32)
    after = (same & (ri > ci)).astype(F32)
    first_half = lax.broadcasted_iota(jnp.int32, (PAIR, 1), 0) < STRETCH

    gram, scores0, keys, keys_t, qs, qscale = [], [], [], [], [], []
    rk_row, rk_col = [], []
    for c in range(blocks):
        sl = slice(c * PAIR, (c + 1) * PAIR)
        k = k_ref[sl, :]
        q = q_ref[sl, :]
        g = mm_t(k, k)
        s = mm_t(q, k)
        gram.append(g)
        scores0.append(s)
        keys.append(k)
        keys_t.append(k.T)
        diag = jnp.where(eye, g, 0.0)
        rk_row.append(lax.rsqrt(jnp.sum(diag, axis=0, keepdims=True) + 1e-06))
        rk_col.append(lax.rsqrt(jnp.sum(diag, axis=1, keepdims=True) + 1e-06))
        qf = q.astype(F32)
        qs.append(qf)
        qscale.append(lax.rsqrt(jnp.sum(qf * qf, axis=1, keepdims=True) + 1e-06) * DK ** (-0.5))

    grow_all, suf_all = [], []
    for c in range(blocks):
        gate = gate_ref[:, c * PAIR:(c + 1) * PAIR]
        grow_all.append(jnp.dot(gate, upto, preferred_element_type=F32, precision=HIGH))
        suf_all.append(jnp.dot(gate, after, preferred_element_type=F32, precision=HIGH))
    head_row = lax.broadcasted_iota(jnp.int32, (gate_ref.shape[0], PAIR), 0)
    items = [(c, r) for r in range(repeat) for c in range(blocks)]
    lower, inv, info = [], [], []
    for c, r in items:
        sl = slice(c * PAIR, (c + 1) * PAIR)
        pick = head_row == h * repeat + r
        grow, suf, rate = [
            jnp.sum(jnp.where(pick, x, 0.0), axis=0, keepdims=True)
            for x in (grow_all[c], suf_all[c], rate_ref[:, sl])
        ]
        stack = jnp.concatenate([grow, suf, rate, jnp.zeros((5, PAIR), F32)], axis=0)
        cols = stack.T
        gcol, sufcol, bcol = cols[:, 0:1], cols[:, 1:2], cols[:, 2:3]
        decay = jnp.exp(jnp.where(causal_mask, gcol - grow, -jnp.inf))
        a = jnp.where(strict_mask, (bcol * rk_col[c]) * gram[c] * rk_row[c] * decay, 0.0)
        sc = scores0[c] * (qscale[c] * rk_row[c]) * decay
        lower.append(a)
        inv.append(jnp.where(eye, 1.0, jnp.where((ri // 2) == (ci // 2), -a, 0.0)))
        info.append((grow, rate, gcol, sufcol, sc))

    size = 2
    while size < STRETCH:
        off = ((ri // (2 * size)) == (ci // (2 * size))) & ((ri // size) != (ci // size))
        invb = [t.astype(BF) for t in inv]
        part = [
            mm(jnp.where(off, a, 0.0).astype(BF), tb).astype(BF) for a, tb in zip(lower, invb)
        ]
        inv = [t - mm(tb, p) for t, tb, p in zip(inv, invb, part)]
        size *= 2

    solved = []
    invb = [t.astype(BF) for t in inv]
    resid = []
    for a, tb in zip(lower, invb):
        hi, lo = split(a)
        resid.append((eye_f - tb.astype(F32)) - (mm(hi, tb) + mm(lo, tb)))
    inv = [tb.astype(F32) + mm(tb, e.astype(BF)) for tb, e in zip(invb, resid)]
    wu = []
    for (c, r), t, (grow, rate, gcol, sufcol, sc) in zip(items, inv, info):
        sl = slice(c * PAIR, (c + 1) * PAIR)
        v = v_ref[sl, r * DV:(r + 1) * DV]
        wh, wl = split(t * (rate * jnp.exp(grow) * rk_row[c]))
        uh, ul = split(t * rate)
        w = mm(wh, keys[c]) + mm(wl, keys[c])
        u = mm(uh, v) + mm(ul, v)
        wu.append((w, u))
    trans, qside = [], []
    for (c, r), (w, u), (grow, rate, gcol, sufcol, sc) in zip(items, wu, info):
        both = jnp.concatenate([w, u], axis=1)
        d = jnp.exp(sufcol) * rk_col[c]
        scaled = both * d
        t0 = mm(keys_t[c], jnp.where(first_half, scaled, 0.0).astype(BF))
        t1 = mm(keys_t[c], jnp.where(first_half, 0.0, scaled).astype(BF))
        sw = mm(sc.astype(BF), both.astype(BF))
        qe = qs[c] * (qscale[c] * jnp.exp(gcol)) - sw[:, :DK]
        trans.append((t0, t1))
        qside.append((qe.astype(BF), sw[:, DK:]))

    finish = []
    begin = []
    total = jnp.int32(0)
    for p in range(prompts):
        begin.append(total)
        total = total + ps_ref[p]
        finish.append(total)

    cl_ref[...] = jnp.zeros_like(cl_ref)
    cm_ref[...] = jnp.zeros_like(cm_ref)
    zero = jnp.zeros((DK, DV), F32)
    states = [jnp.concatenate([zero, eye_f], axis=1) for _ in range(repeat)]
    for n in range(number):
        c, half = n // 2, n % 2
        opens = begin[0] == base + n
        for p in range(1, prompts):
            opens = opens | (begin[p] == base + n)
        closing = jnp.int32(-1)
        for p in range(prompts):
            closing = jnp.where(finish[p] == base + n + 1, jnp.int32(p), closing)
        keep = jnp.where(opens, 0.0, 1.0).astype(F32)
        following = []
        for r in range(repeat):
            i = r * blocks + c
            x = states[r] * keep
            xb = x.astype(BF)
            hs = slice(half * STRETCH, (half + 1) * STRETCH)
            rs = slice(n * STRETCH, (n + 1) * STRETCH)
            qe, su = qside[i]
            oy = mm(qe[hs], xb)
            cs = slice(r * DV, (r + 1) * DV)
            o_ref[rs, cs] = oy[:, :DV] + su[hs]
            y_ref[rs, cs] = oy[:, DV:].astype(BF)
            t = trans[i][half]
            last = (half + 1) * STRETCH - 1
            retain = jnp.exp(info[i][0][:, last:last + 1])
            moved = retain * x - mm(t[:, :DK].astype(BF), xb)
            following.append(
                jnp.concatenate([moved[:, :DV] + t[:, DK:], moved[:, DV:]], axis=1)
            )
        states = following

        @pl.when(closing >= 0)
        def _(following=following, closing=closing):
            for r in range(repeat):
                cl_ref[closing, r] = following[r][:, :DV]
                cm_ref[closing, r] = following[r][:, DV:].astype(BF)

    for r in range(repeat):
        l_ref[r] = states[r][:, :DV]
        m_ref[r] = states[r][:, DV:].astype(BF)


def local_part(queries, key_vectors, values, gate_log, write_rate, prompt_stretches, decode_owner):
    rows = queries.shape[0]
    heads = gate_log.shape[0]
    groups = queries.shape[1] // DK
    repeat = heads // groups
    prompts = prompt_stretches.shape[0]
    whole = pl.BlockSpec((heads, rows), lambda h: (0, 0))
    wide = pl.BlockSpec((rows, repeat * DV), lambda h: (0, h))
    return pl.pallas_call(
        functools.partial(local_kernel, repeat, prompts),
        grid=(groups,),
        in_specs=[
            pl.BlockSpec(memory_space=pltpu.SMEM),
            pl.BlockSpec(memory_space=pltpu.SMEM),
            pl.BlockSpec((rows, DK), lambda h: (0, h)),
            pl.BlockSpec((rows, DK), lambda h: (0, h)),
            wide,
            whole,
            whole,
        ],
        out_specs=[
            wide,
            wide,
            pl.BlockSpec((repeat, DK, DV), lambda h: (h, 0, 0)),
            pl.BlockSpec((repeat, DK, DK), lambda h: (h, 0, 0)),
            pl.BlockSpec((prompts, repeat, DK, DV), lambda h: (0, h, 0, 0)),
            pl.BlockSpec((prompts, repeat, DK, DK), lambda h: (0, h, 0, 0)),
            pl.BlockSpec((2 * prompts, 1, DV), lambda h: (0, 0, 0)),
        ],
        out_shape=[
            jax.ShapeDtypeStruct((rows, heads * DV), F32),
            jax.ShapeDtypeStruct((rows, heads * DV), BF),
            jax.ShapeDtypeStruct((heads, DK, DV), F32),
            jax.ShapeDtypeStruct((heads, DK, DK), BF),
            jax.ShapeDtypeStruct((prompts, heads, DK, DV), F32),
            jax.ShapeDtypeStruct((prompts, heads, DK, DK), BF),
            jax.ShapeDtypeStruct((2 * prompts, 1, DV), F32),
        ],
        compiler_params=pltpu.CompilerParams(vmem_limit_bytes=60 * 1024 * 1024),
    )(prompt_stretches, decode_owner, queries, key_vectors, values, gate_log, write_rate)


def tail_kernel(
    heads, prompts, devices, groups,
    l_ref, m_ref, mask_ref, gain_ref, o_hbm, y_hbm, cl_hbm, cm_hbm, w_hbm,
    mixed_ref, owned_ref,
    o_ref, y_ref, cl_ref, cm_ref, w_ref, inc, nxt, pair_out, pair_in, own,
    up_in, up_out, down_in, down_out, sel_out, sel_in, hid, core_out, core_in, x_out, x_in,
    load_sem, chain_s, chain_r, pair_s, pair_r, up_s, up_r, down_s, down_r,
    sel_s, sel_r, core_s, core_r, x_s, x_r,
):
    pos = lax.axis_index("seq")
    head = lax.axis_index("head")
    xs = groups // 2
    here, core = head // 2, lax.rem(head, 2)
    side = lax.rem(pos, 2)
    mate = pos + 1 - 2 * side
    right, left = lax.rem(pos + 1, devices), lax.rem(pos + devices - 1, devices)
    above, below = lax.rem(pos + 2, devices), lax.rem(pos + devices - 2, devices)
    cols = w_ref.shape[1] // groups

    loads = [
        pltpu.make_async_copy(src, dst, load_sem.at[i])
        for i, (src, dst) in enumerate(
            [(cl_hbm, cl_ref), (cm_hbm, cm_ref), (o_hbm, o_ref), (y_hbm, y_ref), (w_hbm, w_ref)]
        )
    ]
    for load in loads:
        load.start()

    barrier = pltpu.get_barrier_semaphore()
    has_left, has_right = pos >= 1, pos <= devices - 2
    has_below, has_above = pos >= 2, pos <= devices - 3
    count = jnp.int32(xs)
    for has, other in (
        (has_left, left), (has_right, right), (has_below, below), (has_above, above)
    ):
        count = count + has.astype(jnp.int32)

        @pl.when(has)
        def _(other=other):
            pl.semaphore_signal(
                barrier, inc=1, device_id={"seq": other}, device_id_type=pl.DeviceIdType.MESH
            )
    x_heads = [lax.rem(here + k, xs) * 2 + core for k in range(1, xs)]
    for other in [here * 2 + 1 - core] + x_heads:
        pl.semaphore_signal(
            barrier, inc=1, device_id={"head": other}, device_id_type=pl.DeviceIdType.MESH
        )
    pl.semaphore_wait(barrier, count)

    def remote(src, dst, send, recv, **where):
        return pltpu.make_async_remote_copy(
            src_ref=src, dst_ref=dst, send_sem=send, recv_sem=recv,
            device_id=where, device_id_type=pl.DeviceIdType.MESH,
        )

    def chain(h):
        return remote(nxt.at[h], inc.at[h], chain_s.at[h], chain_r.at[h], seq=right)

    def pair(i, h):
        return remote(
            pair_out.at[i, h], pair_in.at[i, h], pair_s.at[i, h], pair_r.at[i, h], seq=mate
        )

    def upward(i, h):
        return remote(up_out.at[i, h], up_in.at[i, h], up_s.at[i, h], up_r.at[i, h], seq=above)

    def downward(i, h):
        return remote(
            down_out.at[i, h], down_in.at[i, h], down_s.at[i, h], down_r.at[i, h], seq=below
        )

    def deliver(h):
        return remote(sel_out.at[h], sel_in.at[h], sel_s.at[h], sel_r.at[h], seq=mate)

    def to_core(k):
        return remote(
            core_out.at[k], core_in.at[k], core_s.at[k], core_r.at[k], head=here * 2 + 1 - core
        )

    def to_x(k):
        return remote(
            x_out.at[k - 1], x_in.at[k - 1], x_s.at[k - 1], x_r.at[k - 1], head=x_heads[k - 1]
        )

    middle = devices // 2
    odd, even = side == 1, side == 0
    last = pos == devices - 1
    low = pos < middle
    pair_sends = [odd | (pos >= middle - 1), odd & low]
    pair_takes = [even | (mate >= middle - 1), even & (mate < middle)]
    up_sends = [has_above, has_above & even]
    up_takes = [has_below, has_below & even]
    down_sends = [has_below, has_below & (odd | low)]
    down_takes = [has_above, has_above & (odd | (pos + 2 < middle))]
    kept_prompt = [1 + side, 3 * side]
    mate_prompt = [2 - side, 3 - 3 * side]

    @pl.when(pos == 0)
    def _():
        inc[...] = jnp.zeros_like(inc)

    for i in range(2):
        @pl.when(jnp.logical_not(up_takes[i]))
        def _(i=i):
            up_in[i] = jnp.zeros(up_in.shape[1:], BF)

        @pl.when(jnp.logical_not(down_takes[i]))
        def _(i=i):
            down_in[i] = jnp.zeros(down_in.shape[1:], BF)

    loads[0].wait()
    loads[1].wait()

    def table(p, h):
        return (cl_ref[p, h] + mm(cm_ref[p, h], inc[h])).astype(BF)

    def table_step(h, _):
        for i in range(2):
            @pl.when(pair_sends[i])
            def _(i=i):
                pair_out[i, h] = table(mate_prompt[i], h)
                pair(i, h).start()

        for i in range(2):
            own[i, h] = table(kept_prompt[i], h)
        return 0

    def chain_step(h, _):
        @pl.when(has_left)
        def _():
            chain(h).wait_recv()

        @pl.when(has_right)
        def _():
            nxt[h] = (mm(m_ref[h], inc[h]) + l_ref[h]).astype(BF)
            chain(h).start()

        @pl.when(last)
        def _():
            table_step(h, 0)

        return 0

    lax.fori_loop(0, heads, chain_step, 0)

    @pl.when(has_right)
    def _():
        lax.fori_loop(0, heads, table_step, 0)

    loads[2].wait()
    loads[3].wait()
    gain = gain_ref[...]
    for j in range(heads):
        cs = slice(j * DV, (j + 1) * DV)
        out = o_ref[:, cs] + mm(y_ref[:, cs], inc[j])
        mean = jnp.mean(out * out, axis=1, keepdims=True)
        hid[:, cs] = (out * lax.rsqrt(mean + 1e-06) * gain).astype(BF)
    loads[4].wait()

    def project(k, which):
        slot = lax.rem(here + k, xs) * 2 + which
        w = w_ref[:, pl.ds(pl.multiple_of(slot * cols, 128), cols)]
        return mm(hid[...], w)

    for k in range(1, xs):
        core_out[k] = project(k, 1 - core).astype(BF)
        to_core(k).start()
    for k in range(1, xs):
        mine = project(k, core)
        to_core(k).wait_recv()
        x_out[k - 1] = (mine + core_in[k].astype(F32)).astype(BF)
        to_x(k).start()

    def gather_step(h, _):
        for i in range(2):
            @pl.when(pair_takes[i])
            def _(i=i):
                pair(i, h).wait_recv()
                own[i, h] = own[i, h] + pair_in[i, h]

        return 0

    def up_step(h, _):
        for i in range(2):
            @pl.when(up_takes[i])
            def _(i=i):
                upward(i, h).wait_recv()

            @pl.when(up_sends[i])
            def _(i=i):
                up_out[i, h] = up_in[i, h] + own[i, h]
                upward(i, h).start()

        return 0

    def down_step(h, _):
        for i in range(2):
            @pl.when(down_takes[i])
            def _(i=i):
                downward(i, h).wait_recv()

            @pl.when(down_sends[i])
            def _(i=i):
                down_out[i, h] = down_in[i, h] + own[i, h]
                downward(i, h).start()

        return 0

    def select_step(h, _):
        kept = jnp.zeros((DK, DV), F32)
        sent = jnp.zeros((DK, DV), F32)
        for i in range(2):
            full = (up_in[i, h] + own[i, h] + down_in[i, h]).astype(F32)
            kept = kept + full * mask_ref[kept_prompt[i]]
            sent = sent + full * mask_ref[prompts + kept_prompt[i]]
        sel_out[h] = sent.astype(BF)
        deliver(h).start()
        owned_ref[0, h] = kept
        return 0

    def both(*steps):
        def run(h, _):
            for step in steps:
                step(h, 0)
            return 0

        lax.fori_loop(0, heads, run, 0)

    @pl.when(low)
    def _():
        both(gather_step, up_step)

    @pl.when(jnp.logical_not(low))
    def _():
        both(gather_step, down_step)

    core_out[0] = project(0, 1 - core).astype(BF)
    to_core(0).start()

    @pl.when(low)
    def _():
        both(down_step, select_step)

    @pl.when(jnp.logical_not(low))
    def _():
        both(up_step, select_step)

    mine = project(0, core)
    to_core(0).wait_recv()
    total = mine + core_in[0].astype(F32)
    for k in range(1, xs):
        to_x(k).wait_recv()
        total = total + x_in[k - 1].astype(F32)
    mixed_ref[...] = total.astype(BF)

    def last_step(h, _):
        deliver(h).wait_recv()
        owned_ref[0, h] = owned_ref[0, h] + sel_in[h].astype(F32)
        deliver(h).wait_send()

        @pl.when(has_right)
        def _():
            chain(h).wait_send()

        for i in range(2):
            for sends, copy in ((pair_sends, pair), (up_sends, upward), (down_sends, downward)):
                @pl.when(sends[i])
                def _(i=i, copy=copy):
                    copy(i, h).wait_send()

        return 0

    lax.fori_loop(0, heads, last_step, 0)
    for k in range(xs):
        to_core(k).wait_send()
    for k in range(1, xs):
        to_x(k).wait_send()


def tail_part(local_state, local_map, masks, norm_gain, o_loc, y_map, close_l, close_m, out_weight):
    rows, width = o_loc.shape
    heads = width // DV
    prompts = close_l.shape[0]
    assert prompts == 4
    devices = lax.axis_size("seq")
    groups = lax.axis_size("head")
    xs = groups // 2
    cols = out_weight.shape[1] // groups
    vmem = pl.BlockSpec(memory_space=pltpu.VMEM)
    anywhere = pl.BlockSpec(memory_space=pl.ANY)
    dma = pltpu.SemaphoreType.DMA
    line = pltpu.VMEM((2, heads, DK, DV), BF)
    state = pltpu.VMEM((heads, DK, DV), BF)
    return pl.pallas_call(
        functools.partial(tail_kernel, heads, prompts, devices, groups),
        in_specs=[vmem] * 4 + [anywhere] * 5,
        out_specs=[vmem, vmem],
        out_shape=[
            jax.ShapeDtypeStruct((rows, cols), BF),
            jax.ShapeDtypeStruct((1, heads, DK, DV), F32),
        ],
        scratch_shapes=[
            pltpu.VMEM(o_loc.shape, F32),
            pltpu.VMEM(y_map.shape, BF),
            pltpu.VMEM(close_l.shape, F32),
            pltpu.VMEM(close_m.shape, BF),
            pltpu.VMEM(out_weight.shape, BF),
            state, state, line, line, line, line, line, line, line, state, state,
            pltpu.VMEM((rows, width), BF),
            pltpu.VMEM((xs, rows, cols), BF),
            pltpu.VMEM((xs, rows, cols), BF),
            pltpu.VMEM((xs - 1, rows, cols), BF),
            pltpu.VMEM((xs - 1, rows, cols), BF),
            dma((5,)),
        ] + [dma((heads,))] * 2 + [dma((2, heads))] * 6 + [dma((heads,))] * 2 + [dma((xs,))] * 2 + [dma((xs - 1,))] * 2,
        compiler_params=pltpu.CompilerParams(
            collective_id=0, has_side_effects=True, vmem_limit_bytes=48 * 1024 * 1024
        ),
    )(
        local_state, local_map, masks, norm_gain.reshape(1, -1),
        o_loc, y_map, close_l, close_m, out_weight,
    )


def body(
    queries, key_vectors, values, gate_log, write_rate,
    prompt_stretches, decode_owner, norm_gain, out_weight,
):
    o_loc, y_map, local_state, local_map, close_l, close_m, masks = local_part(
        queries, key_vectors, values, gate_log, write_rate, prompt_stretches, decode_owner
    )
    return tail_part(
        local_state, local_map, masks, norm_gain, o_loc, y_map, close_l, close_m, out_weight
    )


def solution(mesh):
    return jax.shard_map(
        body,
        mesh=mesh,
        in_specs=(
            P("seq", "head"),
            P("seq", "head"),
            P("seq", "head"),
            P("head", "seq"),
            P("head", "seq"),
            P(),
            P(),
            P(),
            P("head", None),
        ),
        out_specs=(P("seq", "head"), P("seq", "head", None, None)),
        check_vma=False,
    )
```

```python
import functools

import jax
import jax.numpy as jnp
from jax import lax
from jax.experimental import pallas as pl
from jax.experimental.pallas import tpu as pltpu
from jax.sharding import PartitionSpec as P

DK = 128
DV = 128
STRETCH = 64
PAIR = 2 * STRETCH
BF = jnp.bfloat16
F32 = jnp.float32
HIGH = lax.Precision.HIGHEST


def mm(a, b):
    return jnp.dot(a, b, preferred_element_type=F32)


def mm_t(a, b):
    return lax.dot_general(a, b, (((1,), (1,)), ((), ())), preferred_element_type=F32)


def split(x):
    high = x.astype(BF)
    return high, (x - high.astype(F32)).astype(BF)


def local_kernel(
    repeat, prompts, ps_ref, owner_ref, q_ref, k_ref, v_ref, gate_ref, rate_ref,
    o_ref, y_ref, l_ref, m_ref, cl_ref, cm_ref, mask_ref,
):
    h = pl.program_id(0)
    rows = q_ref.shape[0]
    number = rows // STRETCH
    blocks = rows // PAIR
    position = lax.axis_index("seq")
    base = position * number
    mate = position + 1 - 2 * lax.rem(position, 2)
    for p in range(prompts):
        for i, place in enumerate((position, mate)):
            owned = jnp.where(owner_ref[p] == place, 1.0, 0.0).astype(F32)
            mask_ref[i * prompts + p] = jnp.full((1, DV), owned, F32)
    ri = lax.broadcasted_iota(jnp.int32, (PAIR, PAIR), 0)
    ci = lax.broadcasted_iota(jnp.int32, (PAIR, PAIR), 1)
    same = (ri // STRETCH) == (ci // STRETCH)
    eye = ri == ci
    strict_mask = same & (ri > ci)
    causal_mask = same & (ri >= ci)
    eye_f = eye.astype(F32)
    upto = (same & (ri <= ci)).astype(F32).astype(BF)
    after = (same & (ri > ci)).astype(F32).astype(BF)
    first_half = lax.broadcasted_iota(jnp.int32, (PAIR, 1), 0) < STRETCH

    gram, scores0, keys, keys_t, qs, qscale = [], [], [], [], [], []
    rk_row, rk_col = [], []
    for c in range(blocks):
        sl = slice(c * PAIR, (c + 1) * PAIR)
        k = k_ref[sl, :]
        q = q_ref[sl, :]
        g = mm_t(k, k)
        s = mm_t(q, k)
        gram.append(g)
        scores0.append(s)
        keys.append(k)
        keys_t.append(k.T)
        diag = jnp.where(eye, g, 0.0)
        rk_row.append(lax.rsqrt(jnp.sum(diag, axis=0, keepdims=True) + 1e-06))
        rk_col.append(lax.rsqrt(jnp.sum(diag, axis=1, keepdims=True) + 1e-06))
        qf = q.astype(F32)
        qs.append(qf)
        qscale.append(lax.rsqrt(jnp.sum(qf * qf, axis=1, keepdims=True) + 1e-06) * DK ** (-0.5))

    grow_all, suf_all = [], []
    sums = jnp.concatenate([upto, after], axis=1)
    for c in range(blocks):
        gate = gate_ref[:, c * PAIR:(c + 1) * PAIR]
        g_hi = gate.astype(BF)
        rest = gate - g_hi.astype(F32)
        g_mid, g_lo = split(rest)
        three = jnp.concatenate([g.astype(F32) for g in (g_hi, g_mid, g_lo)], axis=0)
        summed = mm(three.astype(BF), sums)
        n_heads = gate.shape[0]
        summed = (
            summed[:n_heads] + summed[n_heads:2 * n_heads] + summed[2 * n_heads:3 * n_heads]
        )
        grow_all.append(summed[:, :PAIR])
        suf_all.append(summed[:, PAIR:])
    head_row = lax.broadcasted_iota(jnp.int32, (gate_ref.shape[0], PAIR), 0)
    items = [(c, r) for r in range(repeat) for c in range(blocks)]
    lower, inv, info = [], [], []
    for c, r in items:
        sl = slice(c * PAIR, (c + 1) * PAIR)
        pick = head_row == h * repeat + r
        grow, suf, rate = [
            jnp.sum(jnp.where(pick, x, 0.0), axis=0, keepdims=True)
            for x in (grow_all[c], suf_all[c], rate_ref[:, sl])
        ]
        stack = jnp.concatenate([grow, suf, rate, jnp.zeros((5, PAIR), F32)], axis=0)
        cols = stack.T
        gcol, sufcol, bcol = cols[:, 0:1], cols[:, 1:2], cols[:, 2:3]
        decay = jnp.exp(jnp.where(causal_mask, gcol - grow, -jnp.inf))
        a = jnp.where(strict_mask, (bcol * rk_col[c]) * gram[c] * rk_row[c] * decay, 0.0)
        sc = scores0[c] * (qscale[c] * rk_row[c]) * decay
        lower.append(a)
        inv.append(jnp.where(eye, 1.0, jnp.where((ri // 2) == (ci // 2), -a, 0.0)))
        info.append((grow, rate, gcol, sufcol, sc))

    lower_b = [a.astype(BF) for a in lower]
    size = 2
    while size < STRETCH:
        off = ((ri // (2 * size)) == (ci // (2 * size))) & ((ri // size) != (ci // size))
        off_b = off.astype(F32).astype(BF)
        invb = [t.astype(BF) for t in inv]
        part = [mm(ab * off_b, tb).astype(BF) for ab, tb in zip(lower_b, invb)]
        inv = [t - mm(tb, p) for t, tb, p in zip(inv, invb, part)]
        size *= 2

    def twice(x, y, x_high=None):
        high = x.astype(BF) if x_high is None else x_high
        low = (x - high.astype(F32)).astype(BF)
        product = mm(jnp.concatenate([high, low], axis=0), y)
        return product[:PAIR] + product[PAIR:]

    invb = [t.astype(BF) for t in inv]
    resid = [
        (eye_f - tb.astype(F32)) - twice(a, tb, ab) for a, ab, tb in zip(lower, lower_b, invb)
    ]
    inv = [tb.astype(F32) + mm(tb, e.astype(BF)) for tb, e in zip(invb, resid)]
    wu = []
    for (c, r), t, (grow, rate, gcol, sufcol, sc) in zip(items, inv, info):
        sl = slice(c * PAIR, (c + 1) * PAIR)
        v = v_ref[sl, r * DV:(r + 1) * DV]
        w = twice(t * (rate * jnp.exp(grow) * rk_row[c]), keys[c])
        u = twice(t * rate, v)
        wu.append((w, u))
    trans, qside = [], []
    for (c, r), (w, u), (grow, rate, gcol, sufcol, sc) in zip(items, wu, info):
        both = jnp.concatenate([w, u], axis=1)
        d = jnp.exp(sufcol) * rk_col[c]
        scaled = both * d
        t0 = mm(keys_t[c], jnp.where(first_half, scaled, 0.0).astype(BF))
        t1 = mm(keys_t[c], jnp.where(first_half, 0.0, scaled).astype(BF))
        sw = mm(sc.astype(BF), both.astype(BF))
        qe = qs[c] * (qscale[c] * jnp.exp(gcol)) - sw[:, :DK]
        trans.append((t0, t1))
        qside.append((qe.astype(BF), sw[:, DK:]))

    finish = []
    begin = []
    total = jnp.int32(0)
    for p in range(prompts):
        begin.append(total)
        total = total + ps_ref[p]
        finish.append(total)

    cl_ref[...] = jnp.zeros_like(cl_ref)
    cm_ref[...] = jnp.zeros_like(cm_ref)
    zero = jnp.zeros((DK, DV), F32)
    states = [jnp.concatenate([zero, eye_f], axis=1) for _ in range(repeat)]
    for n in range(number):
        c, half = n // 2, n % 2
        opens = begin[0] == base + n
        for p in range(1, prompts):
            opens = opens | (begin[p] == base + n)
        closing = jnp.int32(-1)
        for p in range(prompts):
            closing = jnp.where(finish[p] == base + n + 1, jnp.int32(p), closing)
        keep = jnp.where(opens, 0.0, 1.0).astype(F32)
        following = []
        for r in range(repeat):
            i = r * blocks + c
            x = states[r] * keep
            xb = x.astype(BF)
            hs = slice(half * STRETCH, (half + 1) * STRETCH)
            rs = slice(n * STRETCH, (n + 1) * STRETCH)
            qe, su = qside[i]
            oy = mm(qe[hs], xb)
            cs = slice(r * DV, (r + 1) * DV)
            o_ref[rs, cs] = oy[:, :DV] + su[hs]
            y_ref[rs, cs] = oy[:, DV:].astype(BF)
            t = trans[i][half]
            last = (half + 1) * STRETCH - 1
            retain = jnp.exp(info[i][0][:, last:last + 1])
            moved = retain * x - mm(t[:, :DK].astype(BF), xb)
            following.append(
                jnp.concatenate([moved[:, :DV] + t[:, DK:], moved[:, DV:]], axis=1)
            )
        states = following

        @pl.when(closing >= 0)
        def _(following=following, closing=closing):
            for r in range(repeat):
                cl_ref[closing, r] = following[r][:, :DV]
                cm_ref[closing, r] = following[r][:, DV:].astype(BF)

    for r in range(repeat):
        l_ref[r] = states[r][:, :DV]
        m_ref[r] = states[r][:, DV:].astype(BF)


def local_part(queries, key_vectors, values, gate_log, write_rate, prompt_stretches, decode_owner):
    rows = queries.shape[0]
    heads = gate_log.shape[0]
    groups = queries.shape[1] // DK
    repeat = heads // groups
    prompts = prompt_stretches.shape[0]
    whole = pl.BlockSpec((heads, rows), lambda h: (0, 0))
    wide = pl.BlockSpec((rows, repeat * DV), lambda h: (0, h))
    return pl.pallas_call(
        functools.partial(local_kernel, repeat, prompts),
        grid=(groups,),
        in_specs=[
            pl.BlockSpec(memory_space=pltpu.SMEM),
            pl.BlockSpec(memory_space=pltpu.SMEM),
            pl.BlockSpec((rows, DK), lambda h: (0, h)),
            pl.BlockSpec((rows, DK), lambda h: (0, h)),
            wide,
            whole,
            whole,
        ],
        out_specs=[
            wide,
            wide,
            pl.BlockSpec((repeat, DK, DV), lambda h: (h, 0, 0)),
            pl.BlockSpec((repeat, DK, DK), lambda h: (h, 0, 0)),
            pl.BlockSpec((prompts, repeat, DK, DV), lambda h: (0, h, 0, 0)),
            pl.BlockSpec((prompts, repeat, DK, DK), lambda h: (0, h, 0, 0)),
            pl.BlockSpec((2 * prompts, 1, DV), lambda h: (0, 0, 0)),
        ],
        out_shape=[
            jax.ShapeDtypeStruct((rows, heads * DV), F32),
            jax.ShapeDtypeStruct((rows, heads * DV), BF),
            jax.ShapeDtypeStruct((heads, DK, DV), F32),
            jax.ShapeDtypeStruct((heads, DK, DK), BF),
            jax.ShapeDtypeStruct((prompts, heads, DK, DV), F32),
            jax.ShapeDtypeStruct((prompts, heads, DK, DK), BF),
            jax.ShapeDtypeStruct((2 * prompts, 1, DV), F32),
        ],
        compiler_params=pltpu.CompilerParams(vmem_limit_bytes=60 * 1024 * 1024),
    )(prompt_stretches, decode_owner, queries, key_vectors, values, gate_log, write_rate)


def tail_kernel(
    heads, prompts, devices, groups,
    l_hbm, m_hbm, mask_hbm, gain_hbm, o_hbm, y_hbm, cl_hbm, cm_hbm, w_hbm,
    mixed_ref, owned_ref,
    l_ref, m_ref, mask_ref, gain_ref, o_ref, y_ref, cl_ref, cm_ref, w_ref, inc, nxt, pair_out, pair_in, own,
    up_in, up_out, down_in, down_out, sel_out, sel_in, hid, core_out, core_in, x_out, x_in,
    load_sem, chain_s, chain_r, pair_s, pair_r, up_s, up_r, down_s, down_r,
    sel_s, sel_r, core_s, core_r, x_s, x_r,
):
    pos = lax.axis_index("seq")
    head = lax.axis_index("head")
    xs = groups // 2
    here, core = head // 2, lax.rem(head, 2)
    side = lax.rem(pos, 2)
    mate = pos + 1 - 2 * side
    right, left = lax.rem(pos + 1, devices), lax.rem(pos + devices - 1, devices)
    above, below = lax.rem(pos + 2, devices), lax.rem(pos + devices - 2, devices)
    cols = w_ref.shape[1] // groups

    loads = [
        pltpu.make_async_copy(src, dst, load_sem.at[i])
        for i, (src, dst) in enumerate(
            [
                (l_hbm, l_ref), (m_hbm, m_ref), (cl_hbm, cl_ref), (cm_hbm, cm_ref),
                (o_hbm, o_ref), (y_hbm, y_ref), (w_hbm, w_ref), (mask_hbm, mask_ref),
                (gain_hbm, gain_ref),
            ]
        )
    ]
    for load in loads:
        load.start()

    barrier = pltpu.get_barrier_semaphore()
    has_left, has_right = pos >= 1, pos <= devices - 2
    has_below, has_above = pos >= 2, pos <= devices - 3
    count = jnp.int32(xs)
    for has, other in (
        (has_left, left), (has_right, right), (has_below, below), (has_above, above)
    ):
        count = count + has.astype(jnp.int32)

        @pl.when(has)
        def _(other=other):
            pl.semaphore_signal(
                barrier, inc=1, device_id={"seq": other}, device_id_type=pl.DeviceIdType.MESH
            )
    x_heads = [lax.rem(here + k, xs) * 2 + core for k in range(1, xs)]
    for other in [here * 2 + 1 - core] + x_heads:
        pl.semaphore_signal(
            barrier, inc=1, device_id={"head": other}, device_id_type=pl.DeviceIdType.MESH
        )
    pl.semaphore_wait(barrier, count)

    def remote(src, dst, send, recv, **where):
        return pltpu.make_async_remote_copy(
            src_ref=src, dst_ref=dst, send_sem=send, recv_sem=recv,
            device_id=where, device_id_type=pl.DeviceIdType.MESH,
        )

    def chain(h):
        return remote(nxt.at[h], inc.at[h], chain_s.at[h], chain_r.at[h], seq=right)

    def pair(i, h):
        return remote(
            pair_out.at[i, h], pair_in.at[i, h], pair_s.at[i, h], pair_r.at[i, h], seq=mate
        )

    def upward(i, h):
        return remote(up_out.at[i, h], up_in.at[i, h], up_s.at[i, h], up_r.at[i, h], seq=above)

    def downward(i, h):
        return remote(
            down_out.at[i, h], down_in.at[i, h], down_s.at[i, h], down_r.at[i, h], seq=below
        )

    def deliver(h):
        return remote(sel_out.at[h], sel_in.at[h], sel_s.at[h], sel_r.at[h], seq=mate)

    def to_core(k):
        return remote(
            core_out.at[k], core_in.at[k], core_s.at[k], core_r.at[k], head=here * 2 + 1 - core
        )

    def to_x(k):
        return remote(
            x_out.at[k - 1], x_in.at[k - 1], x_s.at[k - 1], x_r.at[k - 1], head=x_heads[k - 1]
        )

    middle = devices // 2
    odd, even = side == 1, side == 0
    last = pos == devices - 1
    low = pos < middle
    pair_sends = [odd | (pos >= middle - 1), odd & low]
    pair_takes = [even | (mate >= middle - 1), even & (mate < middle)]
    up_sends = [has_above, has_above & even]
    up_takes = [has_below, has_below & even]
    down_sends = [has_below, has_below & (odd | low)]
    down_takes = [has_above, has_above & (odd | (pos + 2 < middle))]
    kept_prompt = [1 + side, 3 * side]
    mate_prompt = [2 - side, 3 - 3 * side]

    @pl.when(pos == 0)
    def _():
        inc[...] = jnp.zeros_like(inc)

    for i in range(2):
        @pl.when(jnp.logical_not(up_takes[i]))
        def _(i=i):
            up_in[i] = jnp.zeros(up_in.shape[1:], BF)

        @pl.when(jnp.logical_not(down_takes[i]))
        def _(i=i):
            down_in[i] = jnp.zeros(down_in.shape[1:], BF)

    loads[0].wait()
    loads[1].wait()

    @pl.when(last)
    def _():
        loads[2].wait()
        loads[3].wait()

    def table(p, h):
        return (cl_ref[p, h] + mm(cm_ref[p, h], inc[h])).astype(BF)

    def table_step(h, _):
        for i in range(2):
            @pl.when(pair_sends[i])
            def _(i=i):
                pair_out[i, h] = table(mate_prompt[i], h)
                pair(i, h).start()

        for i in range(2):
            own[i, h] = table(kept_prompt[i], h)
        return 0

    def chain_step(h, _):
        @pl.when(has_left)
        def _():
            chain(h).wait_recv()

        @pl.when(has_right)
        def _():
            nxt[h] = (mm(m_ref[h], inc[h]) + l_ref[h]).astype(BF)
            chain(h).start()

        @pl.when(last)
        def _():
            table_step(h, 0)
            down_out[1, h] = own[1, h]
            downward(1, h).start()

        return 0

    lax.fori_loop(0, heads, chain_step, 0)

    @pl.when(has_right)
    def _():
        loads[2].wait()
        loads[3].wait()
        lax.fori_loop(0, heads, table_step, 0)

    for load in loads[4:6] + loads[7:]:
        load.wait()
    gain = gain_ref[...]
    for j in range(heads):
        cs = slice(j * DV, (j + 1) * DV)
        out = o_ref[:, cs] + mm(y_ref[:, cs], inc[j])
        mean = jnp.mean(out * out, axis=1, keepdims=True)
        hid[:, cs] = (out * lax.rsqrt(mean + 1e-06) * gain).astype(BF)
    def project(k, which):
        slot = lax.rem(here + k, xs) * 2 + which
        w = w_ref[:, pl.ds(pl.multiple_of(slot * cols, 128), cols)]
        return mm(hid[...], w)

    def gather_step(h, _):
        for i in range(2):
            @pl.when(pair_takes[i])
            def _(i=i):
                pair(i, h).wait_recv()
                own[i, h] = own[i, h] + pair_in[i, h]

        return 0

    def up_step(h, _):
        for i in range(2):
            @pl.when(up_takes[i])
            def _(i=i):
                upward(i, h).wait_recv()

            @pl.when(up_sends[i])
            def _(i=i):
                up_out[i, h] = up_in[i, h] + own[i, h]
                upward(i, h).start()

        return 0

    def down_step(h, _):
        for i in range(2):
            @pl.when(down_takes[i])
            def _(i=i):
                downward(i, h).wait_recv()

            @pl.when(down_sends[i] & (has_right if i == 1 else has_below))
            def _(i=i):
                down_out[i, h] = down_in[i, h] + own[i, h]
                downward(i, h).start()

        return 0

    def select_step(h, _):
        kept = jnp.zeros((DK, DV), F32)
        sent = jnp.zeros((DK, DV), F32)
        for i in range(2):
            full = (up_in[i, h] + own[i, h] + down_in[i, h]).astype(F32)
            kept = kept + full * mask_ref[kept_prompt[i]]
            sent = sent + full * mask_ref[prompts + kept_prompt[i]]
        sel_out[h] = sent.astype(BF)
        deliver(h).start()
        owned_ref[0, h] = kept
        return 0

    def both(*steps):
        def run(h, _):
            for step in steps:
                step(h, 0)
            return 0

        lax.fori_loop(0, heads, run, 0)

    @pl.when(low)
    def _():
        both(gather_step, up_step)

    @pl.when(jnp.logical_not(low))
    def _():
        both(gather_step, down_step)

    loads[6].wait()
    for k in range(1, xs):
        core_out[k] = project(k, 1 - core).astype(BF)
        to_core(k).start()
    for k in range(1, xs):
        mine = project(k, core)
        to_core(k).wait_recv()
        x_out[k - 1] = (mine + core_in[k].astype(F32)).astype(BF)
        to_x(k).start()

    core_out[0] = project(0, 1 - core).astype(BF)
    to_core(0).start()

    @pl.when(low)
    def _():
        both(down_step, select_step)

    @pl.when(jnp.logical_not(low))
    def _():
        both(up_step, select_step)

    mine = project(0, core)
    to_core(0).wait_recv()
    total = mine + core_in[0].astype(F32)
    for k in range(1, xs):
        to_x(k).wait_recv()
        total = total + x_in[k - 1].astype(F32)
    mixed_ref[...] = total.astype(BF)

    def last_step(h, _):
        deliver(h).wait_recv()
        owned_ref[0, h] = owned_ref[0, h] + sel_in[h].astype(F32)
        deliver(h).wait_send()

        @pl.when(has_right)
        def _():
            chain(h).wait_send()

        for i in range(2):
            for sends, copy in ((pair_sends, pair), (up_sends, upward), (down_sends, downward)):
                @pl.when(sends[i])
                def _(i=i, copy=copy):
                    copy(i, h).wait_send()

        return 0

    lax.fori_loop(0, heads, last_step, 0)
    for k in range(xs):
        to_core(k).wait_send()
    for k in range(1, xs):
        to_x(k).wait_send()


def tail_part(local_state, local_map, masks, norm_gain, o_loc, y_map, close_l, close_m, out_weight):
    rows, width = o_loc.shape
    heads = width // DV
    prompts = close_l.shape[0]
    assert prompts == 4
    devices = lax.axis_size("seq")
    groups = lax.axis_size("head")
    xs = groups // 2
    cols = out_weight.shape[1] // groups
    vmem = pl.BlockSpec(memory_space=pltpu.VMEM)
    anywhere = pl.BlockSpec(memory_space=pl.ANY)
    dma = pltpu.SemaphoreType.DMA
    line = pltpu.VMEM((2, heads, DK, DV), BF)
    state = pltpu.VMEM((heads, DK, DV), BF)
    return pl.pallas_call(
        functools.partial(tail_kernel, heads, prompts, devices, groups),
        in_specs=[anywhere] * 9,
        out_specs=[vmem, vmem],
        out_shape=[
            jax.ShapeDtypeStruct((rows, cols), BF),
            jax.ShapeDtypeStruct((1, heads, DK, DV), F32),
        ],
        scratch_shapes=[
            pltpu.VMEM(local_state.shape, F32),
            pltpu.VMEM(local_map.shape, BF),
            pltpu.VMEM(masks.shape, F32),
            pltpu.VMEM((1, DV), F32),
            pltpu.VMEM(o_loc.shape, F32),
            pltpu.VMEM(y_map.shape, BF),
            pltpu.VMEM(close_l.shape, F32),
            pltpu.VMEM(close_m.shape, BF),
            pltpu.VMEM(out_weight.shape, BF),
            state, state, line, line, line, line, line, line, line, state, state,
            pltpu.VMEM((rows, width), BF),
            pltpu.VMEM((xs, rows, cols), BF),
            pltpu.VMEM((xs, rows, cols), BF),
            pltpu.VMEM((xs - 1, rows, cols), BF),
            pltpu.VMEM((xs - 1, rows, cols), BF),
            dma((9,)),
        ] + [dma((heads,))] * 2 + [dma((2, heads))] * 6 + [dma((heads,))] * 2 + [dma((xs,))] * 2 + [dma((xs - 1,))] * 2,
        compiler_params=pltpu.CompilerParams(
            collective_id=0, has_side_effects=True, vmem_limit_bytes=60 * 1024 * 1024
        ),
    )(
        local_state, local_map, masks, norm_gain.reshape(1, -1),
        o_loc, y_map, close_l, close_m, out_weight,
    )


def body(
    queries, key_vectors, values, gate_log, write_rate,
    prompt_stretches, decode_owner, norm_gain, out_weight,
):
    o_loc, y_map, local_state, local_map, close_l, close_m, masks = local_part(
        queries, key_vectors, values, gate_log, write_rate, prompt_stretches, decode_owner
    )
    return tail_part(
        local_state, local_map, masks, norm_gain, o_loc, y_map, close_l, close_m, out_weight
    )


def solution(mesh):
    return jax.shard_map(
        body,
        mesh=mesh,
        in_specs=(
            P("seq", "head"),
            P("seq", "head"),
            P("seq", "head"),
            P("head", "seq"),
            P("head", "seq"),
            P(),
            P(),
            P(),
            P("head", None),
        ),
        out_specs=(P("seq", "head"), P("seq", "head", None, None)),
        check_vma=False,
    )
```

```python
import functools

import jax
import jax.numpy as jnp
from jax import lax
from jax.experimental import pallas as pl
from jax.experimental.pallas import tpu as pltpu
from jax.sharding import PartitionSpec as P

DK = 128
DV = 128
STRETCH = 64
PAIR = 2 * STRETCH
BF = jnp.bfloat16
F32 = jnp.float32
HIGH = lax.Precision.HIGHEST


def mm(a, b):
    return jnp.dot(a, b, preferred_element_type=F32)


def mm_t(a, b):
    return lax.dot_general(a, b, (((1,), (1,)), ((), ())), preferred_element_type=F32)


def split(x):
    high = x.astype(BF)
    return high, (x - high.astype(F32)).astype(BF)


def local_kernel(
    repeat, prompts, ps_ref, owner_ref, q_ref, k_ref, v_ref, gate_ref, rate_ref,
    o_ref, y_ref, l_ref, m_ref, cl_ref, cm_ref, mask_ref,
):
    h = pl.program_id(0)
    rows = q_ref.shape[0]
    number = rows // STRETCH
    blocks = rows // PAIR
    position = lax.axis_index("seq")
    base = position * number
    mate = position + 1 - 2 * lax.rem(position, 2)
    for p in range(prompts):
        for i, place in enumerate((position, mate)):
            owned = jnp.where(owner_ref[p] == place, 1.0, 0.0).astype(F32)
            mask_ref[i * prompts + p] = jnp.full((1, DV), owned, F32)
    ri = lax.broadcasted_iota(jnp.int32, (PAIR, PAIR), 0)
    ci = lax.broadcasted_iota(jnp.int32, (PAIR, PAIR), 1)
    same = (ri // STRETCH) == (ci // STRETCH)
    eye = ri == ci
    strict_mask = same & (ri > ci)
    causal_mask = same & (ri >= ci)
    eye_f = eye.astype(F32)
    upto = (same & (ri <= ci)).astype(F32).astype(BF)
    after = (same & (ri > ci)).astype(F32).astype(BF)
    first_half = lax.broadcasted_iota(jnp.int32, (PAIR, 1), 0) < STRETCH

    gram, scores0, keys, keys_t, qs, qscale = [], [], [], [], [], []
    rk_row, rk_col = [], []
    for c in range(blocks):
        sl = slice(c * PAIR, (c + 1) * PAIR)
        k = k_ref[sl, :]
        q = q_ref[sl, :]
        g = mm_t(k, k)
        s = mm_t(q, k)
        gram.append(g)
        scores0.append(s)
        keys.append(k)
        keys_t.append(k.T)
        diag = jnp.where(eye, g, 0.0)
        rk_row.append(lax.rsqrt(jnp.sum(diag, axis=0, keepdims=True) + 1e-06))
        rk_col.append(lax.rsqrt(jnp.sum(diag, axis=1, keepdims=True) + 1e-06))
        qf = q.astype(F32)
        qs.append(qf)
        qscale.append(lax.rsqrt(jnp.sum(qf * qf, axis=1, keepdims=True) + 1e-06) * DK ** (-0.5))

    grow_all, suf_all = [], []
    sums = jnp.concatenate([upto, after], axis=1)
    for c in range(blocks):
        gate = gate_ref[:, c * PAIR:(c + 1) * PAIR]
        g_hi = gate.astype(BF)
        rest = gate - g_hi.astype(F32)
        g_mid, g_lo = split(rest)
        three = jnp.concatenate([g.astype(F32) for g in (g_hi, g_mid, g_lo)], axis=0)
        summed = mm(three.astype(BF), sums)
        n_heads = gate.shape[0]
        summed = (
            summed[:n_heads] + summed[n_heads:2 * n_heads] + summed[2 * n_heads:3 * n_heads]
        )
        grow_all.append(summed[:, :PAIR])
        suf_all.append(summed[:, PAIR:])
    head_row = lax.broadcasted_iota(jnp.int32, (gate_ref.shape[0], PAIR), 0)
    items = [(c, r) for r in range(repeat) for c in range(blocks)]
    lower, inv, info = [], [], []
    for c, r in items:
        sl = slice(c * PAIR, (c + 1) * PAIR)
        pick = head_row == h * repeat + r
        grow, suf, rate = [
            jnp.sum(jnp.where(pick, x, 0.0), axis=0, keepdims=True)
            for x in (grow_all[c], suf_all[c], rate_ref[:, sl])
        ]
        stack = jnp.concatenate([grow, suf, rate, jnp.zeros((5, PAIR), F32)], axis=0)
        cols = stack.T
        gcol, sufcol, bcol = cols[:, 0:1], cols[:, 1:2], cols[:, 2:3]
        decay = jnp.exp(jnp.where(causal_mask, gcol - grow, -jnp.inf))
        a = jnp.where(strict_mask, (bcol * rk_col[c]) * gram[c] * rk_row[c] * decay, 0.0)
        sc = scores0[c] * (qscale[c] * rk_row[c]) * decay
        lower.append(a)
        inv.append(jnp.where(eye, 1.0, jnp.where((ri // 2) == (ci // 2), -a, 0.0)))
        info.append((grow, rate, gcol, sufcol, sc))

    lower_b = [a.astype(BF) for a in lower]
    size = 2
    while size < STRETCH:
        off = ((ri // (2 * size)) == (ci // (2 * size))) & ((ri // size) != (ci // size))
        off_b = off.astype(F32).astype(BF)
        invb = [t.astype(BF) for t in inv]
        part = [mm(ab * off_b, tb).astype(BF) for ab, tb in zip(lower_b, invb)]
        inv = [t - mm(tb, p) for t, tb, p in zip(inv, invb, part)]
        size *= 2

    def twice(x, y, x_high=None):
        high = x.astype(BF) if x_high is None else x_high
        low = (x - high.astype(F32)).astype(BF)
        product = mm(jnp.concatenate([high, low], axis=0), y)
        return product[:PAIR] + product[PAIR:]

    invb = [t.astype(BF) for t in inv]
    resid = [
        (eye_f - tb.astype(F32)) - twice(a, tb, ab) for a, ab, tb in zip(lower, lower_b, invb)
    ]
    inv = [tb.astype(F32) + mm(tb, e.astype(BF)) for tb, e in zip(invb, resid)]
    wu = []
    for (c, r), t, (grow, rate, gcol, sufcol, sc) in zip(items, inv, info):
        sl = slice(c * PAIR, (c + 1) * PAIR)
        v = v_ref[sl, r * DV:(r + 1) * DV]
        w = twice(t * (rate * jnp.exp(grow) * rk_row[c]), keys[c])
        u = twice(t * rate, v)
        wu.append((w, u))
    trans, qside = [], []
    for (c, r), (w, u), (grow, rate, gcol, sufcol, sc) in zip(items, wu, info):
        both = jnp.concatenate([w, u], axis=1)
        d = jnp.exp(sufcol) * rk_col[c]
        scaled = both * d
        t0 = mm(keys_t[c], jnp.where(first_half, scaled, 0.0).astype(BF))
        t1 = mm(keys_t[c], jnp.where(first_half, 0.0, scaled).astype(BF))
        sw = mm(sc.astype(BF), both.astype(BF))
        qe = qs[c] * (qscale[c] * jnp.exp(gcol)) - sw[:, :DK]
        trans.append((t0, t1))
        qside.append((qe.astype(BF), sw[:, DK:]))

    finish = []
    begin = []
    total = jnp.int32(0)
    for p in range(prompts):
        begin.append(total)
        total = total + ps_ref[p]
        finish.append(total)

    cl_ref[...] = jnp.zeros_like(cl_ref)
    cm_ref[...] = jnp.zeros_like(cm_ref)
    zero = jnp.zeros((DK, DV), F32)
    states = [jnp.concatenate([zero, eye_f], axis=1) for _ in range(repeat)]
    for n in range(number):
        c, half = n // 2, n % 2
        opens = begin[0] == base + n
        for p in range(1, prompts):
            opens = opens | (begin[p] == base + n)
        closing = jnp.int32(-1)
        for p in range(prompts):
            closing = jnp.where(finish[p] == base + n + 1, jnp.int32(p), closing)
        keep = jnp.where(opens, 0.0, 1.0).astype(F32)
        following = []
        for r in range(repeat):
            i = r * blocks + c
            x = states[r] * keep
            xb = x.astype(BF)
            hs = slice(half * STRETCH, (half + 1) * STRETCH)
            rs = slice(n * STRETCH, (n + 1) * STRETCH)
            qe, su = qside[i]
            oy = mm(qe[hs], xb)
            cs = slice(r * DV, (r + 1) * DV)
            o_ref[rs, cs] = oy[:, :DV] + su[hs]
            y_ref[rs, cs] = oy[:, DV:].astype(BF)
            t = trans[i][half]
            last = (half + 1) * STRETCH - 1
            retain = jnp.exp(info[i][0][:, last:last + 1])
            moved = retain * x - mm(t[:, :DK].astype(BF), xb)
            following.append(
                jnp.concatenate([moved[:, :DV] + t[:, DK:], moved[:, DV:]], axis=1)
            )
        states = following

        @pl.when(closing >= 0)
        def _(following=following, closing=closing):
            for r in range(repeat):
                cl_ref[closing, r] = following[r][:, :DV]
                cm_ref[closing, r] = following[r][:, DV:].astype(BF)

    for r in range(repeat):
        l_ref[r] = states[r][:, :DV]
        m_ref[r] = states[r][:, DV:].astype(BF)


def local_part(queries, key_vectors, values, gate_log, write_rate, prompt_stretches, decode_owner):
    rows = queries.shape[0]
    heads = gate_log.shape[0]
    groups = queries.shape[1] // DK
    repeat = heads // groups
    prompts = prompt_stretches.shape[0]
    whole = pl.BlockSpec((heads, rows), lambda h: (0, 0))
    wide = pl.BlockSpec((rows, repeat * DV), lambda h: (0, h))
    return pl.pallas_call(
        functools.partial(local_kernel, repeat, prompts),
        grid=(groups,),
        in_specs=[
            pl.BlockSpec(memory_space=pltpu.SMEM),
            pl.BlockSpec(memory_space=pltpu.SMEM),
            pl.BlockSpec((rows, DK), lambda h: (0, h)),
            pl.BlockSpec((rows, DK), lambda h: (0, h)),
            wide,
            whole,
            whole,
        ],
        out_specs=[
            wide,
            wide,
            pl.BlockSpec((repeat, DK, DV), lambda h: (h, 0, 0)),
            pl.BlockSpec((repeat, DK, DK), lambda h: (h, 0, 0)),
            pl.BlockSpec((prompts, repeat, DK, DV), lambda h: (0, h, 0, 0)),
            pl.BlockSpec((prompts, repeat, DK, DK), lambda h: (0, h, 0, 0)),
            pl.BlockSpec((2 * prompts, 1, DV), lambda h: (0, 0, 0)),
        ],
        out_shape=[
            jax.ShapeDtypeStruct((rows, heads * DV), F32),
            jax.ShapeDtypeStruct((rows, heads * DV), BF),
            jax.ShapeDtypeStruct((heads, DK, DV), F32),
            jax.ShapeDtypeStruct((heads, DK, DK), BF),
            jax.ShapeDtypeStruct((prompts, heads, DK, DV), F32),
            jax.ShapeDtypeStruct((prompts, heads, DK, DK), BF),
            jax.ShapeDtypeStruct((2 * prompts, 1, DV), F32),
        ],
        compiler_params=pltpu.CompilerParams(vmem_limit_bytes=60 * 1024 * 1024),
    )(prompt_stretches, decode_owner, queries, key_vectors, values, gate_log, write_rate)


def tail_kernel(
    heads, prompts, devices, groups,
    l_hbm, m_hbm, mask_hbm, gain_hbm, o_hbm, y_hbm, cl_hbm, cm_hbm, w_hbm,
    mixed_ref, owned_ref,
    l_ref, m_ref, mask_ref, gain_ref, o_ref, y_ref, cl_ref, cm_ref, w_ref, inc, nxt, pair_out, pair_in, own,
    up_in, up_out, down_in, down_out, sel_out, sel_in, hid, core_out, core_in, x_out, x_in,
    load_sem, chain_s, chain_r, pair_s, pair_r, up_s, up_r, down_s, down_r,
    sel_s, sel_r, core_s, core_r, x_s, x_r,
):
    pos = lax.axis_index("seq")
    head = lax.axis_index("head")
    xs = groups // 2
    here, core = head // 2, lax.rem(head, 2)
    side = lax.rem(pos, 2)
    mate = pos + 1 - 2 * side
    right, left = lax.rem(pos + 1, devices), lax.rem(pos + devices - 1, devices)
    above, below = lax.rem(pos + 2, devices), lax.rem(pos + devices - 2, devices)
    cols = w_ref.shape[1] // groups

    loads = [
        pltpu.make_async_copy(src, dst, load_sem.at[i])
        for i, (src, dst) in enumerate(
            [
                (l_hbm, l_ref), (m_hbm, m_ref), (cl_hbm, cl_ref), (cm_hbm, cm_ref),
                (o_hbm, o_ref), (y_hbm, y_ref), (w_hbm, w_ref), (mask_hbm, mask_ref),
                (gain_hbm, gain_ref),
            ]
        )
    ]
    for load in loads:
        load.start()

    barrier = pltpu.get_barrier_semaphore()
    has_left, has_right = pos >= 1, pos <= devices - 2
    has_below, has_above = pos >= 2, pos <= devices - 3
    count = jnp.int32(xs)
    for has, other in (
        (has_left, left), (has_right, right), (has_below, below), (has_above, above)
    ):
        count = count + has.astype(jnp.int32)

        @pl.when(has)
        def _(other=other):
            pl.semaphore_signal(
                barrier, inc=1, device_id={"seq": other}, device_id_type=pl.DeviceIdType.MESH
            )
    x_heads = [lax.rem(here + k, xs) * 2 + core for k in range(1, xs)]
    for other in [here * 2 + 1 - core] + x_heads:
        pl.semaphore_signal(
            barrier, inc=1, device_id={"head": other}, device_id_type=pl.DeviceIdType.MESH
        )
    pl.semaphore_wait(barrier, count)

    def remote(src, dst, send, recv, **where):
        return pltpu.make_async_remote_copy(
            src_ref=src, dst_ref=dst, send_sem=send, recv_sem=recv,
            device_id=where, device_id_type=pl.DeviceIdType.MESH,
        )

    def chain(h):
        return remote(nxt.at[h], inc.at[h], chain_s.at[h], chain_r.at[h], seq=right)

    def pair(i, h):
        return remote(
            pair_out.at[i, h], pair_in.at[i, h], pair_s.at[i, h], pair_r.at[i, h], seq=mate
        )

    def upward(i, h):
        return remote(up_out.at[i, h], up_in.at[i, h], up_s.at[i, h], up_r.at[i, h], seq=above)

    def downward(i, h):
        return remote(
            down_out.at[i, h], down_in.at[i, h], down_s.at[i, h], down_r.at[i, h], seq=below
        )

    def deliver(h):
        return remote(sel_out.at[h], sel_in.at[h], sel_s.at[h], sel_r.at[h], seq=mate)

    def to_core(k):
        return remote(
            core_out.at[k], core_in.at[k], core_s.at[k], core_r.at[k], head=here * 2 + 1 - core
        )

    def to_x(k):
        return remote(
            x_out.at[k - 1], x_in.at[k - 1], x_s.at[k - 1], x_r.at[k - 1], head=x_heads[k - 1]
        )

    middle = devices // 2
    odd, even = side == 1, side == 0
    last = pos == devices - 1
    low = pos < middle
    pair_sends = [odd | (pos >= middle - 1), odd & low]
    pair_takes = [even | (mate >= middle - 1), even & (mate < middle)]
    up_sends = [has_above, has_above & even]
    up_takes = [has_below, has_below & even]
    down_sends = [has_below, has_below & (odd | low)]
    down_takes = [has_above, has_above & (odd | (pos + 2 < middle))]
    kept_prompt = [1 + side, 3 * side]
    mate_prompt = [2 - side, 3 - 3 * side]

    @pl.when(pos == 0)
    def _():
        inc[...] = jnp.zeros_like(inc)

    for i in range(2):
        @pl.when(jnp.logical_not(up_takes[i]))
        def _(i=i):
            up_in[i] = jnp.zeros(up_in.shape[1:], BF)

        @pl.when(jnp.logical_not(down_takes[i]))
        def _(i=i):
            down_in[i] = jnp.zeros(down_in.shape[1:], BF)

    loads[0].wait()
    loads[1].wait()

    @pl.when(last)
    def _():
        loads[2].wait()
        loads[3].wait()

    def table(p, h):
        return (cl_ref[p, h] + mm(cm_ref[p, h], inc[h])).astype(BF)

    def table_step(h, _):
        for i in range(2):
            @pl.when(pair_sends[i])
            def _(i=i):
                pair_out[i, h] = table(mate_prompt[i], h)
                pair(i, h).start()

        for i in range(2):
            own[i, h] = table(kept_prompt[i], h)
        return 0

    def chain_step(h, _):
        @pl.when(has_left)
        def _():
            chain(h).wait_recv()

        @pl.when(has_right)
        def _():
            nxt[h] = (mm(m_ref[h], inc[h]) + l_ref[h]).astype(BF)
            chain(h).start()

        @pl.when(last)
        def _():
            table_step(h, 0)
            down_out[1, h] = own[1, h]
            downward(1, h).start()

        return 0

    lax.fori_loop(0, heads, chain_step, 0)

    @pl.when(has_right)
    def _():
        loads[2].wait()
        loads[3].wait()
        lax.fori_loop(0, heads, table_step, 0)

    for load in loads[4:]:
        load.wait()
    gain = gain_ref[...]
    for j in range(heads):
        cs = slice(j * DV, (j + 1) * DV)
        out = o_ref[:, cs] + mm(y_ref[:, cs], inc[j])
        mean = jnp.mean(out * out, axis=1, keepdims=True)
        hid[:, cs] = (out * lax.rsqrt(mean + 1e-06) * gain).astype(BF)
    def project(k, which):
        slot = lax.rem(here + k, xs) * 2 + which
        w = w_ref[:, pl.ds(pl.multiple_of(slot * cols, 128), cols)]
        return mm(hid[...], w)

    def gather_step(h, _):
        for i in range(2):
            @pl.when(pair_takes[i])
            def _(i=i):
                pair(i, h).wait_recv()
                own[i, h] = own[i, h] + pair_in[i, h]

        return 0

    def up_step(h, _):
        for i in range(2):
            @pl.when(up_takes[i])
            def _(i=i):
                upward(i, h).wait_recv()

            @pl.when(up_sends[i])
            def _(i=i):
                up_out[i, h] = up_in[i, h] + own[i, h]
                upward(i, h).start()

        return 0

    def down_step(h, _):
        for i in range(2):
            @pl.when(down_takes[i])
            def _(i=i):
                downward(i, h).wait_recv()

            @pl.when(down_sends[i] & (has_right if i == 1 else has_below))
            def _(i=i):
                down_out[i, h] = down_in[i, h] + own[i, h]
                downward(i, h).start()

        return 0

    def select_step(h, _):
        kept = jnp.zeros((DK, DV), F32)
        sent = jnp.zeros((DK, DV), F32)
        for i in range(2):
            full = (up_in[i, h] + own[i, h] + down_in[i, h]).astype(F32)
            kept = kept + full * mask_ref[kept_prompt[i]]
            sent = sent + full * mask_ref[prompts + kept_prompt[i]]
        sel_out[h] = sent.astype(BF)
        deliver(h).start()
        owned_ref[0, h] = kept
        return 0

    def both(*steps):
        def run(h, _):
            for step in steps:
                step(h, 0)
            return 0

        lax.fori_loop(0, heads, run, 0)

    up_first = pos < devices - 2
    for k in range(1, xs):
        core_out[k] = project(k, 1 - core).astype(BF)
        to_core(k).start()

    @pl.when(up_first)
    def _():
        both(gather_step, up_step)

    @pl.when(jnp.logical_not(up_first))
    def _():
        both(gather_step, down_step)

    for k in range(1, xs):
        mine = project(k, core)
        to_core(k).wait_recv()
        x_out[k - 1] = (mine + core_in[k].astype(F32)).astype(BF)
        to_x(k).start()
    core_out[0] = project(0, 1 - core).astype(BF)
    to_core(0).start()

    @pl.when(up_first)
    def _():
        both(down_step, select_step)

    @pl.when(jnp.logical_not(up_first))
    def _():
        both(up_step, select_step)

    mine = project(0, core)
    to_core(0).wait_recv()
    total = mine + core_in[0].astype(F32)
    for k in range(1, xs):
        to_x(k).wait_recv()
        total = total + x_in[k - 1].astype(F32)
    mixed_ref[...] = total.astype(BF)

    def last_step(h, _):
        deliver(h).wait_recv()
        owned_ref[0, h] = owned_ref[0, h] + sel_in[h].astype(F32)
        deliver(h).wait_send()

        @pl.when(has_right)
        def _():
            chain(h).wait_send()

        for i in range(2):
            for sends, copy in ((pair_sends, pair), (up_sends, upward), (down_sends, downward)):
                @pl.when(sends[i])
                def _(i=i, copy=copy):
                    copy(i, h).wait_send()

        return 0

    lax.fori_loop(0, heads, last_step, 0)
    for k in range(xs):
        to_core(k).wait_send()
    for k in range(1, xs):
        to_x(k).wait_send()


def tail_part(local_state, local_map, masks, norm_gain, o_loc, y_map, close_l, close_m, out_weight):
    rows, width = o_loc.shape
    heads = width // DV
    prompts = close_l.shape[0]
    assert prompts == 4
    devices = lax.axis_size("seq")
    groups = lax.axis_size("head")
    xs = groups // 2
    cols = out_weight.shape[1] // groups
    vmem = pl.BlockSpec(memory_space=pltpu.VMEM)
    anywhere = pl.BlockSpec(memory_space=pl.ANY)
    dma = pltpu.SemaphoreType.DMA
    line = pltpu.VMEM((2, heads, DK, DV), BF)
    state = pltpu.VMEM((heads, DK, DV), BF)
    return pl.pallas_call(
        functools.partial(tail_kernel, heads, prompts, devices, groups),
        in_specs=[anywhere] * 9,
        out_specs=[vmem, vmem],
        out_shape=[
            jax.ShapeDtypeStruct((rows, cols), BF),
            jax.ShapeDtypeStruct((1, heads, DK, DV), F32),
        ],
        scratch_shapes=[
            pltpu.VMEM(local_state.shape, F32),
            pltpu.VMEM(local_map.shape, BF),
            pltpu.VMEM(masks.shape, F32),
            pltpu.VMEM((1, DV), F32),
            pltpu.VMEM(o_loc.shape, F32),
            pltpu.VMEM(y_map.shape, BF),
            pltpu.VMEM(close_l.shape, F32),
            pltpu.VMEM(close_m.shape, BF),
            pltpu.VMEM(out_weight.shape, BF),
            state, state, line, line, line, line, line, line, line, state, state,
            pltpu.VMEM((rows, width), BF),
            pltpu.VMEM((xs, rows, cols), BF),
            pltpu.VMEM((xs, rows, cols), BF),
            pltpu.VMEM((xs - 1, rows, cols), BF),
            pltpu.VMEM((xs - 1, rows, cols), BF),
            dma((9,)),
        ] + [dma((heads,))] * 2 + [dma((2, heads))] * 6 + [dma((heads,))] * 2 + [dma((xs,))] * 2 + [dma((xs - 1,))] * 2,
        compiler_params=pltpu.CompilerParams(
            collective_id=0, has_side_effects=True, vmem_limit_bytes=60 * 1024 * 1024
        ),
    )(
        local_state, local_map, masks, norm_gain.reshape(1, -1),
        o_loc, y_map, close_l, close_m, out_weight,
    )


def copy_kernel(a_ref, b_ref, a_out, b_out, sems):
    copies = [
        pltpu.make_async_copy(a_ref, a_out, sems.at[0]),
        pltpu.make_async_copy(b_ref, b_out, sems.at[1]),
    ]
    for copy in copies:
        copy.start()
    for copy in copies:
        copy.wait()


def copied(a, b):
    anywhere = pl.BlockSpec(memory_space=pl.ANY)
    return pl.pallas_call(
        copy_kernel,
        in_specs=[anywhere, anywhere],
        out_specs=[anywhere, anywhere],
        out_shape=[jax.ShapeDtypeStruct(a.shape, a.dtype), jax.ShapeDtypeStruct(b.shape, b.dtype)],
        scratch_shapes=[pltpu.SemaphoreType.DMA((2,))],
        compiler_params=pltpu.CompilerParams(vmem_limit_bytes=60 * 1024 * 1024),
    )(a, b)


def body(
    queries, key_vectors, values, gate_log, write_rate,
    prompt_stretches, decode_owner, norm_gain, out_weight,
):
    o_loc, y_map, local_state, local_map, close_l, close_m, masks = local_part(
        queries, key_vectors, values, gate_log, write_rate, prompt_stretches, decode_owner
    )
    mixed, owned = tail_part(
        local_state, local_map, masks, norm_gain, o_loc, y_map, close_l, close_m, out_weight
    )
    return copied(mixed, owned)


def solution(mesh):
    return jax.shard_map(
        body,
        mesh=mesh,
        in_specs=(
            P("seq", "head"),
            P("seq", "head"),
            P("seq", "head"),
            P("head", "seq"),
            P("head", "seq"),
            P(),
            P(),
            P(),
            P("head", None),
        ),
        out_specs=(P("seq", "head"), P("seq", "head", None, None)),
        check_vma=False,
    )
```

```python
import functools

import jax
import jax.numpy as jnp
from jax import lax
from jax.experimental import pallas as pl
from jax.experimental.pallas import tpu as pltpu
from jax.sharding import PartitionSpec as P

DK = 128
DV = 128
STRETCH = 64
PAIR = 2 * STRETCH
BF = jnp.bfloat16
F32 = jnp.float32
HIGH = lax.Precision.HIGHEST


def mm(a, b):
    return jnp.dot(a, b, preferred_element_type=F32)


def mm_t(a, b):
    return lax.dot_general(a, b, (((1,), (1,)), ((), ())), preferred_element_type=F32)


def split(x):
    high = x.astype(BF)
    return high, (x - high.astype(F32)).astype(BF)


def local_kernel(
    repeat, prompts, ps_ref, owner_ref, q_ref, k_ref, v_ref, gate_ref, rate_ref,
    o_ref, y_ref, l_ref, m_ref, cl_ref, cm_ref, mask_ref,
):
    h = pl.program_id(0)
    rows = q_ref.shape[0]
    number = rows // STRETCH
    blocks = rows // PAIR
    position = lax.axis_index("seq")
    base = position * number
    mate = position + 1 - 2 * lax.rem(position, 2)
    for p in range(prompts):
        for i, place in enumerate((position, mate)):
            owned = jnp.where(owner_ref[p] == place, 1.0, 0.0).astype(F32)
            mask_ref[i * prompts + p] = jnp.full((1, DV), owned, F32)
    ri = lax.broadcasted_iota(jnp.int32, (PAIR, PAIR), 0)
    ci = lax.broadcasted_iota(jnp.int32, (PAIR, PAIR), 1)
    same = (ri // STRETCH) == (ci // STRETCH)
    eye = ri == ci
    strict_mask = same & (ri > ci)
    causal_mask = same & (ri >= ci)
    eye_f = eye.astype(F32)
    upto = (same & (ri <= ci)).astype(F32).astype(BF)
    after = (same & (ri > ci)).astype(F32).astype(BF)
    first_half = lax.broadcasted_iota(jnp.int32, (PAIR, 1), 0) < STRETCH

    gram, scores0, keys, keys_t, qs, qscale = [], [], [], [], [], []
    rk_row, rk_col = [], []
    for c in range(blocks):
        sl = slice(c * PAIR, (c + 1) * PAIR)
        k = k_ref[sl, :]
        q = q_ref[sl, :]
        g = mm_t(k, k)
        s = mm_t(q, k)
        gram.append(g)
        scores0.append(s)
        keys.append(k)
        keys_t.append(k.T)
        diag = jnp.where(eye, g, 0.0)
        rk_row.append(lax.rsqrt(jnp.sum(diag, axis=0, keepdims=True) + 1e-06))
        rk_col.append(lax.rsqrt(jnp.sum(diag, axis=1, keepdims=True) + 1e-06))
        qf = q.astype(F32)
        qs.append(qf)
        qscale.append(lax.rsqrt(jnp.sum(qf * qf, axis=1, keepdims=True) + 1e-06) * DK ** (-0.5))

    grow_all, suf_all = [], []
    sums = jnp.concatenate([upto, after], axis=1)
    for c in range(blocks):
        gate = gate_ref[:, c * PAIR:(c + 1) * PAIR]
        g_hi = gate.astype(BF)
        rest = gate - g_hi.astype(F32)
        g_mid, g_lo = split(rest)
        three = jnp.concatenate([g.astype(F32) for g in (g_hi, g_mid, g_lo)], axis=0)
        summed = mm(three.astype(BF), sums)
        n_heads = gate.shape[0]
        summed = (
            summed[:n_heads] + summed[n_heads:2 * n_heads] + summed[2 * n_heads:3 * n_heads]
        )
        grow_all.append(summed[:, :PAIR])
        suf_all.append(summed[:, PAIR:])
    head_row = lax.broadcasted_iota(jnp.int32, (gate_ref.shape[0], PAIR), 0)
    items = [(c, r) for r in range(repeat) for c in range(blocks)]
    lower, inv, info = [], [], []
    for c, r in items:
        sl = slice(c * PAIR, (c + 1) * PAIR)
        pick = head_row == h * repeat + r
        grow, suf, rate = [
            jnp.sum(jnp.where(pick, x, 0.0), axis=0, keepdims=True)
            for x in (grow_all[c], suf_all[c], rate_ref[:, sl])
        ]
        stack = jnp.concatenate([grow, suf, rate, jnp.zeros((5, PAIR), F32)], axis=0)
        cols = stack.T
        gcol, sufcol, bcol = cols[:, 0:1], cols[:, 1:2], cols[:, 2:3]
        decay = jnp.exp(jnp.where(causal_mask, gcol - grow, -jnp.inf))
        a = jnp.where(strict_mask, (bcol * rk_col[c]) * gram[c] * rk_row[c] * decay, 0.0)
        sc = scores0[c] * (qscale[c] * rk_row[c]) * decay
        lower.append(a)
        inv.append(jnp.where(eye, 1.0, jnp.where((ri // 2) == (ci // 2), -a, 0.0)))
        info.append((grow, rate, gcol, sufcol, sc))

    lower_b = [a.astype(BF) for a in lower]
    size = 2
    while size < STRETCH:
        off = ((ri // (2 * size)) == (ci // (2 * size))) & ((ri // size) != (ci // size))
        off_b = off.astype(F32).astype(BF)
        invb = [t.astype(BF) for t in inv]
        part = [mm(ab * off_b, tb).astype(BF) for ab, tb in zip(lower_b, invb)]
        inv = [t - mm(tb, p) for t, tb, p in zip(inv, invb, part)]
        size *= 2

    def twice(x, y, x_high=None):
        high = x.astype(BF) if x_high is None else x_high
        low = (x - high.astype(F32)).astype(BF)
        product = mm(jnp.concatenate([high, low], axis=0), y)
        return product[:PAIR] + product[PAIR:]

    invb = [t.astype(BF) for t in inv]
    resid = [
        (eye_f - tb.astype(F32)) - twice(a, tb, ab) for a, ab, tb in zip(lower, lower_b, invb)
    ]
    inv = [tb.astype(F32) + mm(tb, e.astype(BF)) for tb, e in zip(invb, resid)]
    wu = []
    for (c, r), t, (grow, rate, gcol, sufcol, sc) in zip(items, inv, info):
        sl = slice(c * PAIR, (c + 1) * PAIR)
        v = v_ref[sl, r * DV:(r + 1) * DV]
        w = twice(t * (rate * jnp.exp(grow) * rk_row[c]), keys[c])
        u = twice(t * rate, v)
        wu.append((w, u))
    trans, qside = [], []
    for (c, r), (w, u), (grow, rate, gcol, sufcol, sc) in zip(items, wu, info):
        both = jnp.concatenate([w, u], axis=1)
        d = jnp.exp(sufcol) * rk_col[c]
        scaled = both * d
        t0 = mm(keys_t[c], jnp.where(first_half, scaled, 0.0).astype(BF))
        t1 = mm(keys_t[c], jnp.where(first_half, 0.0, scaled).astype(BF))
        sw = mm(sc.astype(BF), both.astype(BF))
        qe = qs[c] * (qscale[c] * jnp.exp(gcol)) - sw[:, :DK]
        trans.append((t0, t1))
        qside.append((qe.astype(BF), sw[:, DK:]))

    finish = []
    begin = []
    total = jnp.int32(0)
    for p in range(prompts):
        begin.append(total)
        total = total + ps_ref[p]
        finish.append(total)

    cl_ref[...] = jnp.zeros_like(cl_ref)
    cm_ref[...] = jnp.zeros_like(cm_ref)
    zero = jnp.zeros((DK, DV), F32)
    states = [jnp.concatenate([zero, eye_f], axis=1) for _ in range(repeat)]
    for n in range(number):
        c, half = n // 2, n % 2
        opens = begin[0] == base + n
        for p in range(1, prompts):
            opens = opens | (begin[p] == base + n)
        closing = jnp.int32(-1)
        for p in range(prompts):
            closing = jnp.where(finish[p] == base + n + 1, jnp.int32(p), closing)
        keep = jnp.where(opens, 0.0, 1.0).astype(F32)
        following = []
        for r in range(repeat):
            i = r * blocks + c
            x = states[r] * keep
            xb = x.astype(BF)
            hs = slice(half * STRETCH, (half + 1) * STRETCH)
            rs = slice(n * STRETCH, (n + 1) * STRETCH)
            qe, su = qside[i]
            oy = mm(qe[hs], xb)
            cs = slice(r * DV, (r + 1) * DV)
            o_ref[rs, cs] = oy[:, :DV] + su[hs]
            y_ref[rs, cs] = oy[:, DV:].astype(BF)
            t = trans[i][half]
            last = (half + 1) * STRETCH - 1
            retain = jnp.exp(info[i][0][:, last:last + 1])
            moved = retain * x - mm(t[:, :DK].astype(BF), xb)
            following.append(
                jnp.concatenate([moved[:, :DV] + t[:, DK:], moved[:, DV:]], axis=1)
            )
        states = following

        @pl.when(closing >= 0)
        def _(following=following, closing=closing):
            for r in range(repeat):
                cl_ref[closing, r] = following[r][:, :DV]
                cm_ref[closing, r] = following[r][:, DV:].astype(BF)

    for r in range(repeat):
        l_ref[r] = states[r][:, :DV]
        m_ref[r] = states[r][:, DV:].astype(BF)


def local_part(queries, key_vectors, values, gate_log, write_rate, prompt_stretches, decode_owner):
    rows = queries.shape[0]
    heads = gate_log.shape[0]
    groups = queries.shape[1] // DK
    repeat = heads // groups
    prompts = prompt_stretches.shape[0]
    whole = pl.BlockSpec((heads, rows), lambda h: (0, 0))
    wide = pl.BlockSpec((rows, repeat * DV), lambda h: (0, h))
    return pl.pallas_call(
        functools.partial(local_kernel, repeat, prompts),
        grid=(groups,),
        in_specs=[
            pl.BlockSpec(memory_space=pltpu.SMEM),
            pl.BlockSpec(memory_space=pltpu.SMEM),
            pl.BlockSpec((rows, DK), lambda h: (0, h)),
            pl.BlockSpec((rows, DK), lambda h: (0, h)),
            wide,
            whole,
            whole,
        ],
        out_specs=[
            wide,
            wide,
            pl.BlockSpec((repeat, DK, DV), lambda h: (h, 0, 0)),
            pl.BlockSpec((repeat, DK, DK), lambda h: (h, 0, 0)),
            pl.BlockSpec((prompts, repeat, DK, DV), lambda h: (0, h, 0, 0)),
            pl.BlockSpec((prompts, repeat, DK, DK), lambda h: (0, h, 0, 0)),
            pl.BlockSpec((2 * prompts, 1, DV), lambda h: (0, 0, 0)),
        ],
        out_shape=[
            jax.ShapeDtypeStruct((rows, heads * DV), F32),
            jax.ShapeDtypeStruct((rows, heads * DV), BF),
            jax.ShapeDtypeStruct((heads, DK, DV), F32),
            jax.ShapeDtypeStruct((heads, DK, DK), BF),
            jax.ShapeDtypeStruct((prompts, heads, DK, DV), F32),
            jax.ShapeDtypeStruct((prompts, heads, DK, DK), BF),
            jax.ShapeDtypeStruct((2 * prompts, 1, DV), F32),
        ],
        compiler_params=pltpu.CompilerParams(vmem_limit_bytes=60 * 1024 * 1024),
    )(prompt_stretches, decode_owner, queries, key_vectors, values, gate_log, write_rate)


def tail_kernel(
    heads, prompts, devices, groups,
    l_hbm, m_hbm, mask_hbm, gain_hbm, o_hbm, y_hbm, cl_hbm, cm_hbm, w_hbm,
    mixed_ref, owned_ref,
    l_ref, m_ref, mask_ref, gain_ref, o_ref, y_ref, cl_ref, cm_ref, w_ref, inc, nxt, pair_out, pair_in, own,
    up_in, up_out, down_in, down_out, sel_out, sel_in, hid, core_out, core_in, x_out, x_in,
    load_sem, chain_s, chain_r, pair_s, pair_r, up_s, up_r, down_s, down_r,
    sel_s, sel_r, core_s, core_r, x_s, x_r,
):
    pos = lax.axis_index("seq")
    head = lax.axis_index("head")
    xs = groups // 2
    here, core = head // 2, lax.rem(head, 2)
    side = lax.rem(pos, 2)
    mate = pos + 1 - 2 * side
    right, left = lax.rem(pos + 1, devices), lax.rem(pos + devices - 1, devices)
    above, below = lax.rem(pos + 2, devices), lax.rem(pos + devices - 2, devices)
    cols = w_ref.shape[1] // groups

    loads = [
        pltpu.make_async_copy(src, dst, load_sem.at[i])
        for i, (src, dst) in enumerate(
            [
                (l_hbm, l_ref), (m_hbm, m_ref), (cl_hbm, cl_ref), (cm_hbm, cm_ref),
                (o_hbm, o_ref), (y_hbm, y_ref), (w_hbm, w_ref), (mask_hbm, mask_ref),
                (gain_hbm, gain_ref),
            ]
        )
    ]
    for load in loads:
        load.start()

    barrier = pltpu.get_barrier_semaphore()
    has_left, has_right = pos >= 1, pos <= devices - 2
    has_below, has_above = pos >= 2, pos <= devices - 3
    count = jnp.int32(xs)
    for has, other in (
        (has_left, left), (has_right, right), (has_below, below), (has_above, above)
    ):
        count = count + has.astype(jnp.int32)

        @pl.when(has)
        def _(other=other):
            pl.semaphore_signal(
                barrier, inc=1, device_id={"seq": other}, device_id_type=pl.DeviceIdType.MESH
            )
    x_heads = [lax.rem(here + k, xs) * 2 + core for k in range(1, xs)]
    for other in [here * 2 + 1 - core] + x_heads:
        pl.semaphore_signal(
            barrier, inc=1, device_id={"head": other}, device_id_type=pl.DeviceIdType.MESH
        )
    pl.semaphore_wait(barrier, count)

    def remote(src, dst, send, recv, **where):
        return pltpu.make_async_remote_copy(
            src_ref=src, dst_ref=dst, send_sem=send, recv_sem=recv,
            device_id=where, device_id_type=pl.DeviceIdType.MESH,
        )

    def chain(h):
        return remote(nxt.at[h], inc.at[h], chain_s.at[h], chain_r.at[h], seq=right)

    def pair(i, h):
        return remote(
            pair_out.at[i, h], pair_in.at[i, h], pair_s.at[i, h], pair_r.at[i, h], seq=mate
        )

    def upward(i, h):
        return remote(up_out.at[i, h], up_in.at[i, h], up_s.at[i, h], up_r.at[i, h], seq=above)

    def downward(i, h):
        return remote(
            down_out.at[i, h], down_in.at[i, h], down_s.at[i, h], down_r.at[i, h], seq=below
        )

    def deliver(h):
        return remote(sel_out.at[h], sel_in.at[h], sel_s.at[h], sel_r.at[h], seq=mate)

    def to_core(k):
        return remote(
            core_out.at[k], core_in.at[k], core_s.at[k], core_r.at[k], head=here * 2 + 1 - core
        )

    def to_x(k):
        return remote(
            x_out.at[k - 1], x_in.at[k - 1], x_s.at[k - 1], x_r.at[k - 1], head=x_heads[k - 1]
        )

    middle = devices // 2
    odd, even = side == 1, side == 0
    last = pos == devices - 1
    low = pos < middle
    pair_sends = [odd | (pos >= middle - 1), odd & low]
    pair_takes = [even | (mate >= middle - 1), even & (mate < middle)]
    up_sends = [has_above, has_above & even]
    up_takes = [has_below, has_below & even]
    down_sends = [has_below, has_below & (odd | low)]
    down_takes = [has_above, has_above & (odd | (pos + 2 < middle))]
    kept_prompt = [1 + side, 3 * side]
    mate_prompt = [2 - side, 3 - 3 * side]

    @pl.when(pos == 0)
    def _():
        inc[...] = jnp.zeros_like(inc)

    for i in range(2):
        @pl.when(jnp.logical_not(up_takes[i]))
        def _(i=i):
            up_in[i] = jnp.zeros(up_in.shape[1:], BF)

        @pl.when(jnp.logical_not(down_takes[i]))
        def _(i=i):
            down_in[i] = jnp.zeros(down_in.shape[1:], BF)

    loads[0].wait()
    loads[1].wait()

    @pl.when(last)
    def _():
        loads[2].wait()
        loads[3].wait()

    def table(p, h):
        return (cl_ref[p, h] + mm(cm_ref[p, h], inc[h])).astype(BF)

    def table_step(h, _):
        for i in range(2):
            @pl.when(pair_sends[i])
            def _(i=i):
                pair_out[i, h] = table(mate_prompt[i], h)
                pair(i, h).start()

        for i in range(2):
            own[i, h] = table(kept_prompt[i], h)
        return 0

    def chain_step(h, _):
        @pl.when(has_left)
        def _():
            chain(h).wait_recv()

        @pl.when(has_right)
        def _():
            nxt[h] = (mm(m_ref[h], inc[h]) + l_ref[h]).astype(BF)
            chain(h).start()

        @pl.when(last)
        def _():
            table_step(h, 0)
            down_out[1, h] = own[1, h]
            downward(1, h).start()

        return 0

    lax.fori_loop(0, heads, chain_step, 0)

    @pl.when(has_right)
    def _():
        loads[2].wait()
        loads[3].wait()
        lax.fori_loop(0, heads, table_step, 0)

    for load in loads[4:]:
        load.wait()
    gain = gain_ref[...]
    for j in range(heads):
        cs = slice(j * DV, (j + 1) * DV)
        out = o_ref[:, cs] + mm(y_ref[:, cs], inc[j])
        mean = jnp.mean(out * out, axis=1, keepdims=True)
        hid[:, cs] = (out * lax.rsqrt(mean + 1e-06) * gain).astype(BF)
    def project(k, which):
        slot = lax.rem(here + k, xs) * 2 + which
        w = w_ref[:, pl.ds(pl.multiple_of(slot * cols, 128), cols)]
        return mm(hid[...], w)

    def gather_step(h, _):
        for i in range(2):
            @pl.when(pair_takes[i])
            def _(i=i):
                pair(i, h).wait_recv()
                own[i, h] = own[i, h] + pair_in[i, h]

        return 0

    def up_step(h, _):
        for i in range(2):
            @pl.when(up_takes[i])
            def _(i=i):
                upward(i, h).wait_recv()

            @pl.when(up_sends[i])
            def _(i=i):
                up_out[i, h] = up_in[i, h] + own[i, h]
                upward(i, h).start()

        return 0

    def down_step(h, _):
        for i in range(2):
            @pl.when(down_takes[i])
            def _(i=i):
                downward(i, h).wait_recv()

            @pl.when(down_sends[i] & (has_right if i == 1 else has_below))
            def _(i=i):
                down_out[i, h] = down_in[i, h] + own[i, h]
                downward(i, h).start()

        return 0

    def select_step(h, _):
        kept = jnp.zeros((DK, DV), F32)
        sent = jnp.zeros((DK, DV), F32)
        for i in range(2):
            full = (up_in[i, h] + own[i, h] + down_in[i, h]).astype(F32)
            kept = kept + full * mask_ref[kept_prompt[i]]
            sent = sent + full * mask_ref[prompts + kept_prompt[i]]
        sel_out[h] = sent.astype(BF)
        deliver(h).start()
        owned_ref[0, h] = kept
        return 0

    def both(*steps):
        def run(h, _):
            for step in steps:
                step(h, 0)
            return 0

        lax.fori_loop(0, heads, run, 0)

    up_first = pos < devices - 2
    for k in range(1, xs):
        core_out[k] = project(k, 1 - core).astype(BF)
        to_core(k).start()

    @pl.when(up_first)
    def _():
        both(gather_step, up_step)

    @pl.when(jnp.logical_not(up_first))
    def _():
        both(gather_step, down_step)

    for k in range(1, xs):
        mine = project(k, core)
        to_core(k).wait_recv()
        x_out[k - 1] = (mine + core_in[k].astype(F32)).astype(BF)
        to_x(k).start()
    core_out[0] = project(0, 1 - core).astype(BF)
    to_core(0).start()

    @pl.when(up_first)
    def _():
        both(down_step, select_step)

    @pl.when(jnp.logical_not(up_first))
    def _():
        both(up_step, select_step)

    mine = project(0, core)
    to_core(0).wait_recv()
    total = mine + core_in[0].astype(F32)
    for k in range(1, xs):
        to_x(k).wait_recv()
        total = total + x_in[k - 1].astype(F32)
    mixed_ref[...] = total.astype(BF)

    def last_step(h, _):
        deliver(h).wait_recv()
        owned_ref[0, h] = owned_ref[0, h] + sel_in[h].astype(F32)
        deliver(h).wait_send()

        @pl.when(has_right)
        def _():
            chain(h).wait_send()

        for i in range(2):
            for sends, copy in ((pair_sends, pair), (up_sends, upward), (down_sends, downward)):
                @pl.when(sends[i])
                def _(i=i, copy=copy):
                    copy(i, h).wait_send()

        return 0

    lax.fori_loop(0, heads, last_step, 0)
    for k in range(xs):
        to_core(k).wait_send()
    for k in range(1, xs):
        to_x(k).wait_send()


def tail_part(local_state, local_map, masks, norm_gain, o_loc, y_map, close_l, close_m, out_weight):
    rows, width = o_loc.shape
    heads = width // DV
    prompts = close_l.shape[0]
    assert prompts == 4
    devices = lax.axis_size("seq")
    groups = lax.axis_size("head")
    xs = groups // 2
    cols = out_weight.shape[1] // groups
    vmem = pl.BlockSpec(memory_space=pltpu.VMEM)
    anywhere = pl.BlockSpec(memory_space=pl.ANY)
    dma = pltpu.SemaphoreType.DMA
    line = pltpu.VMEM((2, heads, DK, DV), BF)
    state = pltpu.VMEM((heads, DK, DV), BF)
    return pl.pallas_call(
        functools.partial(tail_kernel, heads, prompts, devices, groups),
        in_specs=[anywhere] * 9,
        out_specs=[vmem, vmem],
        out_shape=[
            jax.ShapeDtypeStruct((rows, cols), BF),
            jax.ShapeDtypeStruct((1, heads, DK, DV), F32),
        ],
        scratch_shapes=[
            pltpu.VMEM(local_state.shape, F32),
            pltpu.VMEM(local_map.shape, BF),
            pltpu.VMEM(masks.shape, F32),
            pltpu.VMEM((1, DV), F32),
            pltpu.VMEM(o_loc.shape, F32),
            pltpu.VMEM(y_map.shape, BF),
            pltpu.VMEM(close_l.shape, F32),
            pltpu.VMEM(close_m.shape, BF),
            pltpu.VMEM(out_weight.shape, BF),
            state, state, line, line, line, line, line, line, line, state, state,
            pltpu.VMEM((rows, width), BF),
            pltpu.VMEM((xs, rows, cols), BF),
            pltpu.VMEM((xs, rows, cols), BF),
            pltpu.VMEM((xs - 1, rows, cols), BF),
            pltpu.VMEM((xs - 1, rows, cols), BF),
            dma((9,)),
        ] + [dma((heads,))] * 2 + [dma((2, heads))] * 6 + [dma((heads,))] * 2 + [dma((xs,))] * 2 + [dma((xs - 1,))] * 2,
        compiler_params=pltpu.CompilerParams(
            collective_id=0, has_side_effects=True, vmem_limit_bytes=60 * 1024 * 1024
        ),
    )(
        local_state, local_map, masks, norm_gain.reshape(1, -1),
        o_loc, y_map, close_l, close_m, out_weight,
    )


def copy_kernel(a_ref, b_ref, a_out, b_out):
    a_out[...] = a_ref[...]
    b_out[...] = b_ref[...]


def copied(a, b):
    specs = [
        pl.BlockSpec((a.shape[0] // 2, a.shape[1]), lambda i: (i, 0)),
        pl.BlockSpec((1, b.shape[1] // 2) + b.shape[2:], lambda i: (0, i, 0, 0)),
    ]
    return pl.pallas_call(
        copy_kernel,
        grid=(2,),
        in_specs=specs,
        out_specs=specs,
        out_shape=[jax.ShapeDtypeStruct(a.shape, a.dtype), jax.ShapeDtypeStruct(b.shape, b.dtype)],
        compiler_params=pltpu.CompilerParams(vmem_limit_bytes=60 * 1024 * 1024),
    )(a, b)


def body(
    queries, key_vectors, values, gate_log, write_rate,
    prompt_stretches, decode_owner, norm_gain, out_weight,
):
    o_loc, y_map, local_state, local_map, close_l, close_m, masks = local_part(
        queries, key_vectors, values, gate_log, write_rate, prompt_stretches, decode_owner
    )
    mixed, owned = tail_part(
        local_state, local_map, masks, norm_gain, o_loc, y_map, close_l, close_m, out_weight
    )
    return copied(mixed, owned)


def solution(mesh):
    return jax.shard_map(
        body,
        mesh=mesh,
        in_specs=(
            P("seq", "head"),
            P("seq", "head"),
            P("seq", "head"),
            P("head", "seq"),
            P("head", "seq"),
            P(),
            P(),
            P(),
            P("head", None),
        ),
        out_specs=(P("seq", "head"), P("seq", "head", None, None)),
        check_vma=False,
    )
```
